32 devices in a mesh: tm: 16 (over z, x, core), sec: 2 (over y).
Axes of the slice: x: 2, y: 2, z: 4, core: 2. Of those that a mesh axis runs over, the one named last changes fastest.
Arguments:
- record: float32 [768, 8192], P('sec', 'tm'), may hold values from -2000 to 2000
- fir_taps: float32 [65], replicated, may hold values from -0.75 to 0.75
- source_index: int32 [16], replicated, may hold values from 0 to 767
Outputs:
- xcorr: float32 [768, 16, 513], P(('sec', 'tm'))
The draws below stay inside these ranges and needn't reach their ends.
All inputs are finite; a program needn't handle non-finite values.
Results may differ from the reference program's by a relative error of at most 0.004.
Values may be sent and summed in bfloat16 or wider, within the bound.
No kernel may reach another device: no remote copies, remote signals or barrier semaphores. Data moves between devices by JAX's collectives and lax.ppermute only.
A program may use at most 320 MiB of HBM per device.

```python
import math
import jax
import jax.numpy as jnp
from jax import lax

CH_BLOCK = 24
SAMPLES = 8192
HALF_LAG = 256
HALF_TAPS = 32
NSRC = 16
TAPS = 65
CHANNELS = 768
N_TM = 16


def draw_record(key, part):
    key = jax.random.fold_in(key, 11)
    key_noise, key_channel, key_time = jax.random.split(key, 3)
    position = jnp.arange(SAMPLES, dtype=jnp.float32) / SAMPLES
    noise = jax.random.truncated_normal(key_noise, -4.0, 4.0, (CHANNELS, SAMPLES), jnp.float32)
    channel_scale = jnp.exp(jax.random.uniform(key_channel, (CHANNELS, 1), jnp.float32, 0.0, math.log(10.0)))
    time_scale = jnp.exp(jax.random.uniform(key_time, (1, SAMPLES), jnp.float32, 0.0, math.log(10.0)))
    time_scale = time_scale * jnp.exp(math.log(3.0) * position)[None, :]
    return noise * channel_scale * time_scale


def set_ends(array, stream_key, smallest, top_value):
    extent = array.shape
    index_at = [jax.random.randint(jax.random.fold_in(stream_key, axis), (), 0, extent[axis]) for axis in range(len(extent))]
    array = array.at[tuple(index_at)].set(smallest)
    longest = extent.index(max(extent))
    index_at[longest] = (index_at[longest] + 1) % extent[longest]
    return array.at[tuple(index_at)].set(top_value)


def centred(rng, dims, scale, limit, kind=jnp.bfloat16):
    values = scale * jax.random.normal(rng, dims, jnp.float32)
    return jnp.clip(values, min=-limit, max=limit).astype(kind)


def setup_inputs(seed: int = 0) -> dict:
    arg_keys = jax.random.split(jax.random.key(seed), 4)
    return {
        "record": draw_record(jax.random.fold_in(arg_keys[3], 71), 0),
        "fir_taps": centred(arg_keys[1], (TAPS,), TAPS ** -0.5, 0.75, jnp.float32),
        "source_index": set_ends(jax.random.randint(arg_keys[2], (NSRC,), 0, CHANNELS), jax.random.fold_in(arg_keys[2], 1), 0, CHANNELS - 1).astype(jnp.int32),
    }


eps = 1e-06
lag_group = 64
time_block = 1024

def unit_rows(rows):
    energy = jnp.sqrt(lax.optimization_barrier(jnp.mean(rows * rows, axis=1)) + eps)
    return (rows / energy[:, None]).astype(jnp.bfloat16)

def toeplitz(piece):
    count, length = piece.shape
    width = length + lag_group + 1
    padded = jnp.concatenate([piece, jnp.zeros((count, lag_group + 1), piece.dtype)], axis=1)
    tiled = jnp.tile(padded, (1, lag_group))[:, :lag_group * (width - 1)]
    return tiled.reshape(count * lag_group, width - 1)

def lag_rows(shifted, start, length, groups):
    pieces = [shifted[:, start + step * lag_group:start + step * lag_group + length + lag_group] for step in range(groups)]
    return jnp.stack(pieces, axis=1).reshape(shifted.shape[0] * groups, length + lag_group)

def correlate(pilots, units):
    nlag = 2 * HALF_LAG + 1
    groups = -(-nlag // lag_group)
    samples = units.shape[1]
    block = min(time_block, samples)
    count = units.shape[0]
    sources = pilots.shape[0]
    shifted = jnp.pad(units, ((0, 0), (HALF_LAG, groups * lag_group - HALF_LAG)))
    total = jnp.zeros((sources * lag_group, count * groups), jnp.float32)
    for start in range(0, samples, block):
        plate = toeplitz(pilots[:, start:start + block]).astype(jnp.float32)
        rows = lag_rows(shifted, start, block, groups).astype(jnp.float32)
        total = total + jnp.dot(plate, rows.T, precision=lax.Precision.HIGHEST)
    result = total.reshape(sources, lag_group, count, groups).transpose(2, 0, 3, 1)
    result = result.reshape(count, sources, groups * lag_group)[:, :, :nlag]
    return result * (1.0 / math.sqrt(samples))

def reference(record, fir_taps, source_index):
    padded = jnp.pad(record, ((HALF_TAPS, HALF_TAPS), (0, 0)))
    filtered = jnp.zeros_like(record)
    for offset in range(2 * HALF_TAPS + 1):
        filtered = filtered + fir_taps[offset] * padded[offset:offset + CHANNELS]
    units = unit_rows(filtered)
    pilots = unit_rows(filtered[source_index])
    sections = units.reshape(CHANNELS // (CH_BLOCK * N_TM), CH_BLOCK * N_TM, SAMPLES)
    result = lax.map(lambda section: correlate(pilots, section), sections)
    return result.reshape(CHANNELS, NSRC, 2 * HALF_LAG + 1)
```

```python
import functools
import math

import jax
import jax.numpy as jnp
from jax import lax
from jax.experimental import pallas as pl
from jax.experimental.pallas import tpu as pltpu
from jax.sharding import PartitionSpec as P

f32 = jnp.float32
bf16 = jnp.bfloat16
HALF_LAG = 256
NLAG = 2 * HALF_LAG + 1
SCALE = 2.0**32
EPS = 1e-6 * SCALE * SCALE
G = 32
HALO = 32
SMEM = pltpu.SMEM
VMEM = pltpu.VMEM


def filter_kernel(index_ref, taps_ref, rec_ref, filt_ref, exch_ref, hi_ref, lo_ref, ext_ref, *, pair):
    rows, width = rec_ref.shape
    taps = taps_ref.shape[0]
    sources = index_ref.shape[0]
    lane = lax.broadcasted_iota(jnp.int32, (8, 256), 1)
    base = jnp.zeros((8, 256), f32)
    for m in range(taps):
        base = jnp.where(lane == m, taps_ref[m] * SCALE, base)
    tall = jnp.concatenate([base] * 16, axis=0)
    band = pltpu.roll(tall, 0, 1, stride=1, stride_axis=0)
    band_hi = band.astype(bf16)
    band_lo = (band - band_hi.astype(f32)).astype(bf16)
    both = jnp.concatenate([band_hi, band_lo], axis=0)
    edge = jnp.zeros((64, width), bf16)
    tiles = -(-(rows + 64) // 128)
    spare = hi_ref.shape[0] - 64 - rows
    for ref in (hi_ref, lo_ref):
        ref[:64, :] = edge
        ref[64 + rows :, :] = jnp.zeros((spare, width), bf16)
    rec = rec_ref[...]
    rec_hi = rec.astype(bf16)
    hi_ref[64 : 64 + rows, :] = rec_hi
    lo_ref[64 : 64 + rows, :] = (rec - rec_hi.astype(f32)).astype(bf16)
    for i in range(tiles):
        hi = hi_ref[128 * i : 128 * i + 256, :]
        lo = lo_ref[128 * i : 128 * i + 256, :]
        big = jnp.dot(both, hi, preferred_element_type=f32)
        small = jnp.dot(band_hi, lo, preferred_element_type=f32)
        ext_ref[128 * i : 128 * i + 128, :] = big[:128] + (big[128:] + small)
    filt_ref[...] = ext_ref[HALO : HALO + rows, :]
    first = lax.axis_index("sec") * rows - HALO
    for s in range(sources):
        row = index_ref[s] - first
        inside = jnp.logical_and(row >= 0, row < rows + 2 * HALO)
        at = jnp.where(inside, row, 0)
        exch_ref[s : s + 1, :] = jnp.where(inside, ext_ref[pl.ds(at, 1), :], 0.0)
    down = ext_ref[:HALO, :]
    up = ext_ref[HALO + rows : 2 * HALO + rows, :]
    if pair:
        exch_ref[sources:, :] = jnp.where(lax.axis_index("sec") == 0, up, down)
    else:
        exch_ref[sources : sources + HALO, :] = down
        exch_ref[sources + HALO :, :] = up


def filter_rows(record, fir_taps, source_index, pair):
    rows, width = record.shape
    sources = source_index.shape[0]
    tiles = -(-(rows + 64) // 128)
    deep = 128 * (tiles + 1)
    return pl.pallas_call(
        functools.partial(filter_kernel, pair=pair),
        out_shape=(
            jax.ShapeDtypeStruct((rows, width), f32),
            jax.ShapeDtypeStruct((sources + HALO * (1 if pair else 2), width), f32),
        ),
        in_specs=[
            pl.BlockSpec(memory_space=SMEM),
            pl.BlockSpec(memory_space=SMEM),
            pl.BlockSpec(memory_space=VMEM),
        ],
        scratch_shapes=[
            pltpu.VMEM((deep, width), bf16),
            pltpu.VMEM((deep, width), bf16),
            pltpu.VMEM((128 * tiles, width), f32),
        ],
        compiler_params=pltpu.CompilerParams(vmem_limit_bytes=24 * 1024 * 1024),
    )(source_index, fir_taps, record)


def pack_kernel(filt_ref, pilots_ref, low_ref, high_ref, out_ref, *, count):
    rows = filt_ref.shape[0]
    pilots = pilots_ref[...].astype(bf16)
    sources = pilots.shape[0]
    for d in range(out_ref.shape[0]):
        out_ref[d, :sources, :] = pilots
        lo, hi = d * count, (d + 1) * count
        part = filt_ref[lo:hi, :]
        if lo < HALO:
            n = min(hi, HALO) - lo
            add = low_ref[lo : lo + n, :]
            part = jnp.concatenate([part[:n] + add, part[n:]], axis=0) if n < count else part + add
        if hi > rows - HALO:
            n = hi - max(lo, rows - HALO)
            add = high_ref[max(lo, rows - HALO) - (rows - HALO) : hi - (rows - HALO), :]
            part = jnp.concatenate([part[: count - n], part[count - n :] + add], axis=0) if n < count else part + add
        out_ref[d, sources:, :] = part.astype(bf16)


def pack(filt, pilots, low, high, devices):
    rows, width = filt.shape
    count = rows // devices
    return pl.pallas_call(
        functools.partial(pack_kernel, count=count),
        out_shape=jax.ShapeDtypeStruct((devices, pilots.shape[0] + count, width), bf16),
        compiler_params=pltpu.CompilerParams(vmem_limit_bytes=24 * 1024 * 1024),
    )(filt, pilots, low, high)


def corr_kernel(x_ref, o_ref, p_ref, z_ref, acc_ref, os_ref, *, kc, count):
    wins, _, win = x_ref.shape
    T=wins*win
    p_ref[:, :128]=jnp.zeros((16,128),p_ref.dtype)
    p_ref[:, 128+T:]=jnp.zeros((16,p_ref.shape[1]-128-T),p_ref.dtype)
    esum=jnp.zeros((16,128),f32)
    usum=jnp.zeros((count,128),f32)
    for w in range(wins):
        pw=x_ref[w,0:16,:]
        p_ref[:,128+w*win:128+(w+1)*win]=pw.astype(p_ref.dtype)
        uw=x_ref[w,16:16+count,:].astype(f32)
        pf=pw.astype(f32)
        for q in range(win//128):
            s=slice(q*128,(q+1)*128)
            esum=esum+pf[:,s]*pf[:,s]; usum=usum+uw[:,s]*uw[:,s]
    nz=z_ref.shape[0]//128
    zero=jnp.zeros((count,128),f32)
    def utile(k):
        k=k-2
        if k<0 or k>=T//128: return zero
        w,q=divmod(k*128,win)
        return x_ref[w,16:16+count,q:q+128].astype(f32)
    lane=lax.broadcasted_iota(jnp.int32,(count,128),1)
    padrows=jnp.zeros((32-count,128),f32)
    rolled=None
    for k in range(nz+1):
        t=utile(k)
        nxt=[t]+[pltpu.roll(t,128-32*r,1) for r in (1,2,3)]
        if rolled is not None:
            parts=[]
            for r in range(4):
                v=rolled[r] if r==0 else jnp.where(lane<128-32*r, rolled[r], nxt[r])
                parts+= [v,padrows]
            blk=jnp.concatenate(parts,axis=0)
            z_ref[(k-1)*128:k*128,:]=blk.T.astype(bf16)
        rolled=nxt
    acc_ref[...]=jnp.zeros_like(acc_ref)
    steps=-(-(T+G)//kc)
    def body(i,_):
        t0=pl.multiple_of(i*kc,kc)
        X=p_ref[:,pl.ds(t0,kc+128)]
        rows=[]
        for j in range(G+1):
            rows.append((pltpu.roll(X,j,1) if j else X)[:,128:].astype(bf16))
        plate=jnp.concatenate(rows,axis=0)
        rhs=jnp.concatenate([z_ref[pl.ds(pl.multiple_of(t0+128*a,128),kc),:] for a in range(4)],axis=1)
        d=jnp.dot(plate,rhs,preferred_element_type=f32)
        for a in range(4): acc_ref[a]+=d[:,128*a:128*a+128]
        return 0
    lax.fori_loop(0,steps,body,0)
    es=lax.rsqrt(jnp.sum(esum,axis=1,keepdims=True)/T+EPS)
    ue=lax.rsqrt(jnp.sum(usum,axis=1,keepdims=True)/T+EPS)/math.sqrt(T)
    lane=lax.broadcasted_iota(jnp.int32,(count,128),1)
    for quad in range(4):
        scl=[jnp.broadcast_to(ue*jnp.broadcast_to(es[4*quad+m:4*quad+m+1],(count,1)),(count,128)) for m in range(4)]
        for a in range(4):
            blk=jnp.concatenate([acc_ref[a,pl.ds(4*quad+m,32,stride=16),:] for m in range(4)],axis=0)
            Y=blk.T
            for m in range(4):
                o=None
                for r in range(4):
                    v=Y[32*r:32*r+count,:]
                    sh=(32*(r-m))%128
                    v=pltpu.roll(v,sh,1) if sh else v
                    o=v if o is None else jnp.where(lane<32*r,o,v)
                os_ref[a,pl.ds(4*quad+m,count,stride=16),:]=o*scl[m]
    last=acc_ref[3,512:528,:]
    last=pltpu.roll(last,32,1)
    last=jnp.concatenate([last*es]+[jnp.zeros((112,128),f32)],axis=0).T[:count]*ue
    for s in range(16):
        v=pltpu.roll(last,(128-s)%128,1) if s else last
        os_ref[4,pl.ds(s,count,stride=16),:]=v
    for a in range(4): o_ref[:,128*a:128*a+128]=os_ref[a]
    o_ref[:,512:513]=os_ref[4][:,0:1]

def correlate(x):
    wins, rows, win = x.shape
    count = rows - 16
    samples = wins * win
    kc = 1664
    steps = -(-(samples + G) // kc)
    out = pl.pallas_call(
        functools.partial(corr_kernel, kc=kc, count=count),
        out_shape=jax.ShapeDtypeStruct((count * 16, NLAG), f32),
        scratch_shapes=[
            pltpu.VMEM((16, steps * kc + 128), bf16),
            pltpu.VMEM((steps * kc + 384, 128), bf16),
            pltpu.VMEM((4, (G + 1) * 16, 128), f32),
            pltpu.VMEM((5, count * 16, 128), f32),
        ],
        compiler_params=pltpu.CompilerParams(vmem_limit_bytes=48 * 1024 * 1024),
    )(x)
    return out.reshape(count, 16, NLAG)


def shards(record, fir_taps, source_index):
    sections = lax.axis_size("sec")
    pair = sections == 2
    sources = source_index.shape[0]
    filt, exch = filter_rows(record, fir_taps, source_index, pair)
    if pair:
        other = lax.ppermute(exch, "sec", [(0, 1), (1, 0)])
        pilots = exch[:sources] + other[:sources]
        here = lax.axis_index("sec")
        edge = other[sources:]
        low = jnp.where(here == 1, edge, 0.0)
        high = jnp.where(here == 0, edge, 0.0)
    else:
        pilots = lax.psum(exch[:sources], "sec")
        up = [(i, i + 1) for i in range(sections - 1)]
        down = [(i + 1, i) for i in range(sections - 1)]
        high = lax.ppermute(exch[sources : sources + HALO], "sec", down)
        low = lax.ppermute(exch[sources + HALO :], "sec", up)
    blocks = pack(filt, pilots, low, high, lax.axis_size("tm"))
    return correlate(lax.all_to_all(blocks, "tm", 0, 0, tiled=True))


def solution(mesh):
    in_specs = (P("sec", "tm"), P(), P())
    out_specs = P(("sec", "tm"), None, None)
    return jax.shard_map(shards, mesh=mesh, in_specs=in_specs, out_specs=out_specs, check_vma=False)
```

```python
import functools
import math

import jax
import jax.numpy as jnp
from jax import lax
from jax.experimental import pallas as pl
from jax.experimental.pallas import tpu as pltpu
from jax.sharding import PartitionSpec as P

f32 = jnp.float32
bf16 = jnp.bfloat16
HALF_LAG = 256
NLAG = 2 * HALF_LAG + 1
SCALE = 2.0**32
EPS = 1e-6 * SCALE * SCALE
G = 32
HALO = 32
SMEM = pltpu.SMEM
VMEM = pltpu.VMEM


def filter_kernel(index_ref, taps_ref, rec_ref, filt_ref, exch_ref, hi_ref, lo_ref, ext_ref, *, pair):
    rows, width = rec_ref.shape
    taps = taps_ref.shape[0]
    sources = index_ref.shape[0]
    lane = lax.broadcasted_iota(jnp.int32, (8, 256), 1)
    base = jnp.zeros((8, 256), f32)
    for m in range(taps):
        base = jnp.where(lane == m, taps_ref[m] * SCALE, base)
    tall = jnp.concatenate([base] * 16, axis=0)
    band = pltpu.roll(tall, 0, 1, stride=1, stride_axis=0)
    band_hi = band.astype(bf16)
    band_lo = (band - band_hi.astype(f32)).astype(bf16)
    both = jnp.concatenate([band_hi, band_lo], axis=0)
    edge = jnp.zeros((64, width), bf16)
    tiles = -(-(rows + 64) // 128)
    spare = hi_ref.shape[0] - 64 - rows
    for ref in (hi_ref, lo_ref):
        ref[:64, :] = edge
        ref[64 + rows :, :] = jnp.zeros((spare, width), bf16)
    rec = rec_ref[...]
    rec_hi = rec.astype(bf16)
    hi_ref[64 : 64 + rows, :] = rec_hi
    lo_ref[64 : 64 + rows, :] = (rec - rec_hi.astype(f32)).astype(bf16)
    for i in range(tiles):
        hi = hi_ref[128 * i : 128 * i + 256, :]
        lo = lo_ref[128 * i : 128 * i + 256, :]
        big = jnp.dot(both, hi, preferred_element_type=f32)
        small = jnp.dot(band_hi, lo, preferred_element_type=f32)
        ext_ref[128 * i : 128 * i + 128, :] = big[:128] + (big[128:] + small)
    filt_ref[...] = ext_ref[HALO : HALO + rows, :]
    first = lax.axis_index("sec") * rows - HALO
    for s in range(sources):
        row = index_ref[s] - first
        inside = jnp.logical_and(row >= 0, row < rows + 2 * HALO)
        at = jnp.where(inside, row, 0)
        exch_ref[s : s + 1, :] = jnp.where(inside, ext_ref[pl.ds(at, 1), :], 0.0)
    down = ext_ref[:HALO, :]
    up = ext_ref[HALO + rows : 2 * HALO + rows, :]
    if pair:
        exch_ref[sources:, :] = jnp.where(lax.axis_index("sec") == 0, up, down)
    else:
        exch_ref[sources : sources + HALO, :] = down
        exch_ref[sources + HALO :, :] = up


def filter_rows(record, fir_taps, source_index, pair):
    rows, width = record.shape
    sources = source_index.shape[0]
    tiles = -(-(rows + 64) // 128)
    deep = 128 * (tiles + 1)
    return pl.pallas_call(
        functools.partial(filter_kernel, pair=pair),
        out_shape=(
            jax.ShapeDtypeStruct((rows, width), f32),
            jax.ShapeDtypeStruct((sources + HALO * (1 if pair else 2), width), f32),
        ),
        in_specs=[
            pl.BlockSpec(memory_space=SMEM),
            pl.BlockSpec(memory_space=SMEM),
            pl.BlockSpec(memory_space=VMEM),
        ],
        scratch_shapes=[
            pltpu.VMEM((deep, width), bf16),
            pltpu.VMEM((deep, width), bf16),
            pltpu.VMEM((128 * tiles, width), f32),
        ],
        compiler_params=pltpu.CompilerParams(vmem_limit_bytes=24 * 1024 * 1024),
    )(source_index, fir_taps, record)


def pack_kernel(filt_ref, pilots_ref, low_ref, high_ref, out_ref, *, count):
    rows = filt_ref.shape[0]
    pilots = pilots_ref[...].astype(bf16)
    sources = pilots.shape[0]
    for d in range(out_ref.shape[0]):
        out_ref[d, :sources, :] = pilots
        lo, hi = d * count, (d + 1) * count
        part = filt_ref[lo:hi, :]
        if lo < HALO:
            n = min(hi, HALO) - lo
            add = low_ref[lo : lo + n, :]
            part = jnp.concatenate([part[:n] + add, part[n:]], axis=0) if n < count else part + add
        if hi > rows - HALO:
            n = hi - max(lo, rows - HALO)
            add = high_ref[max(lo, rows - HALO) - (rows - HALO) : hi - (rows - HALO), :]
            part = jnp.concatenate([part[: count - n], part[count - n :] + add], axis=0) if n < count else part + add
        out_ref[d, sources:, :] = part.astype(bf16)


def pack(filt, pilots, low, high, devices):
    rows, width = filt.shape
    count = rows // devices
    return pl.pallas_call(
        functools.partial(pack_kernel, count=count),
        out_shape=jax.ShapeDtypeStruct((devices, pilots.shape[0] + count, width), bf16),
        compiler_params=pltpu.CompilerParams(vmem_limit_bytes=24 * 1024 * 1024),
    )(filt, pilots, low, high)


def corr_kernel(x_ref, o_ref, lo_ref, v_ref, z_ref, acc_ref, *, kc, count):
    wins, _, win = x_ref.shape
    T=wins*win
    KT=T+256
    nt=T//128
    per=win//128
    esum=jnp.zeros((16,128),f32)
    usum=jnp.zeros((count,128),f32)
    zlo=jnp.zeros((16,256),bf16)
    lo_ref[:,:256]=zlo
    lo_ref[:,256+T:]=zlo[:,:128]
    v_ref[:,:128]=zlo[:,:128]
    v_ref[:,256+T:]=zlo[:,:128]
    lane8=lax.broadcasted_iota(jnp.int32,(8,128),1)
    def him(a,b):
        return jnp.concatenate([a,jnp.where(lane8<112,pltpu.roll(a,112,1),pltpu.roll(b,112,1))],axis=0).astype(bf16)
    z8=jnp.zeros((8,128),f32)
    prev=z8
    for k in range(nt):
        w,q=divmod(k,per); s=slice(q*128,q*128+128)
        p=x_ref[w,0:16,s].astype(f32)
        u=x_ref[w,16:16+count,s].astype(f32)
        esum=esum+p*p; usum=usum+u*u
        lo_ref[:,256+128*k:384+128*k]=x_ref[w,16:32,s]
        v_ref[:,128+128*k:256+128*k]=him(prev,u[16:])
        prev=u[16:]
    v_ref[:,128+T:256+T]=him(prev,z8)
    lane=lax.broadcasted_iota(jnp.int32,(16,128),1)
    zp=jnp.zeros((16,128),bf16)
    for q in range(4): z_ref[q,:,:512]=jnp.zeros((16,512),bf16)
    def ptile(k):
        if k>=nt: return zp
        w,q=divmod(k,per)
        return x_ref[w,0:16,q*128:q*128+128]
    state=[[zp]*4,[zp]*4]
    def zbuild(k):
        t=ptile(k)
        rolls=[t]+[pltpu.roll(t,32*q,1) for q in (1,2,3)]
        S=[t]+[jnp.where(lane<32*q,state[0][q],rolls[q]) for q in (1,2,3)]
        for q in range(4): z_ref[q,:,512+128*k:640+128*k]=S[q]
        state[0]=rolls; state[1]=S
    steps=-(-KT//kc)
    def chunk(t0,first):
        X=lo_ref[:,pl.ds(t0,kc+128)]
        V=v_ref[:,pl.ds(t0,kc+128)]
        w=kc+128
        rows=[(pltpu.roll(X,w-j,1) if j else X)[:,:kc] for j in range(G+1)]
        rows+=[(pltpu.roll(V,w-j,1) if j else V)[:,:kc] for j in range(G//2)]
        rows.append(pltpu.roll(V,w-16,1)[:,:kc])
        plate=jnp.concatenate(rows,axis=0)
        rhs=jnp.concatenate([z_ref[g%4,:,pl.ds(t0+512-128*(g//4),kc)] for g in range(16)],axis=0)
        d=lax.dot_general(plate,rhs,(((1,),(1,)),((),())),preferred_element_type=f32)
        for a in range(2):
            if first: acc_ref[a]=d[:,128*a:128*a+128]
            else: acc_ref[a]+=d[:,128*a:128*a+128]
    for i in range(steps):
        for k in range(i*kc//128,(i+1)*kc//128): zbuild(k)
        chunk(i*kc,i==0)
    es=lax.rsqrt(jnp.sum(esum,axis=1,keepdims=True)/T+EPS)
    ue=lax.rsqrt(jnp.sum(usum,axis=1,keepdims=True)/T+EPS)/math.sqrt(T)
    esb=jnp.broadcast_to(es,(16,128))
    hi0=16*(G+1)
    def lags(h,c):
        if c<16: return acc_ref[h,pl.ds(c,32,stride=16),:]
        return jnp.concatenate([acc_ref[h,pl.ds(hi0+c-16,16,stride=16),:],acc_ref[h,pl.ds(hi0+c-8,16,stride=16),:]],axis=0)
    for quad in range(count//4):
        scl=[esb*jnp.broadcast_to(ue[4*quad+m:4*quad+m+1],(16,128)) for m in range(4)]
        for h in range(2):
            Y=jnp.concatenate([lags(h,4*quad+m) for m in range(4)],axis=0).T
            for b in range(2):
                for m in range(4):
                    o=None
                    for q in range(4):
                        v=Y[64*b+16*q:64*b+16*q+16,:]
                        sh=(32*(q-m))%128
                        v=pltpu.roll(v,sh,1) if sh else v
                        o=v if o is None else jnp.where(lane<32*q,o,v)
                    o_ref[4*quad+m,:,(2*h+b)*128:(2*h+b)*128+128]=o*scl[m]
    last=jnp.concatenate([acc_ref[1,512:528,:],acc_ref[1,hi0+264:hi0+272,:]],axis=0)
    last=jnp.concatenate([last*ue,jnp.zeros((104,128),f32)],axis=0).T[112:128]*es
    for c in range(count):
        v=pltpu.roll(last,128-c,1) if c else last
        o_ref[c,:,512:513]=v[:,0:1]
def correlate(x,kc=2816):
    wins,rows,win=x.shape
    count=rows-16
    T=wins*win
    out=pl.pallas_call(functools.partial(corr_kernel,kc=kc,count=count),
        out_shape=jax.ShapeDtypeStruct((count,16,NLAG),f32),
        scratch_shapes=[pltpu.VMEM((16,T+384),bf16),pltpu.VMEM((16,T+384),bf16),pltpu.VMEM((4,16,T+768),bf16),pltpu.VMEM((2,16*(3*G//2+2),128),f32)],
        compiler_params=pltpu.CompilerParams(vmem_limit_bytes=48*1024*1024),
    )(x)
    return out


def shards(record, fir_taps, source_index):
    sections = lax.axis_size("sec")
    pair = sections == 2
    sources = source_index.shape[0]
    filt, exch = filter_rows(record, fir_taps, source_index, pair)
    if pair:
        other = lax.ppermute(exch, "sec", [(0, 1), (1, 0)])
        pilots = exch[:sources] + other[:sources]
        here = lax.axis_index("sec")
        edge = other[sources:]
        low = jnp.where(here == 1, edge, 0.0)
        high = jnp.where(here == 0, edge, 0.0)
    else:
        pilots = lax.psum(exch[:sources], "sec")
        up = [(i, i + 1) for i in range(sections - 1)]
        down = [(i + 1, i) for i in range(sections - 1)]
        high = lax.ppermute(exch[sources : sources + HALO], "sec", down)
        low = lax.ppermute(exch[sources + HALO :], "sec", up)
    blocks = pack(filt, pilots, low, high, lax.axis_size("tm"))
    return correlate(lax.all_to_all(blocks, "tm", 0, 0, tiled=True))


def solution(mesh):
    in_specs = (P("sec", "tm"), P(), P())
    out_specs = P(("sec", "tm"), None, None)
    return jax.shard_map(shards, mesh=mesh, in_specs=in_specs, out_specs=out_specs, check_vma=False)
```

```python
import functools
import math

import jax
import jax.numpy as jnp
from jax import lax
from jax.experimental import pallas as pl
from jax.experimental.pallas import tpu as pltpu
from jax.sharding import PartitionSpec as P

f32 = jnp.float32
bf16 = jnp.bfloat16
HALF_LAG = 256
NLAG = 2 * HALF_LAG + 1
SCALE = 2.0**32
EPS = 1e-6 * SCALE * SCALE
G = 32
HALO = 32
FETCHES = 3
VMEM_ALL = 64 * 1024 * 1024


def band_halves(taps_ref, shift):
    lane = lax.broadcasted_iota(jnp.int32, (8, 256), 1)
    base = jnp.zeros((8, 256), f32)
    for m in range(taps_ref.shape[0]):
        base = jnp.where(lane == m, taps_ref[m] * SCALE, base)
    tall = jnp.concatenate([base] * 16, axis=0)
    band = pltpu.roll(tall, shift, 1, stride=1, stride_axis=0)
    high = band.astype(bf16)
    return high, (band - high.astype(f32)).astype(bf16)


def clear_edges(refs, rows):
    for ref in refs:
        deep, width = ref.shape
        ref[:64, :] = jnp.zeros((64, width), bf16)
        ref[64 + rows :, :] = jnp.zeros((deep - 64 - rows, width), bf16)


def split_rows(rec, hi_ref, lo_ref, at):
    high = rec.astype(bf16)
    hi_ref[at : at + rec.shape[0], :] = high
    lo_ref[at : at + rec.shape[0], :] = (rec - high.astype(f32)).astype(bf16)


def band_product(band, hi_ref, lo_ref, i):
    hi = hi_ref[128 * i : 128 * i + 256, :]
    lo = lo_ref[128 * i : 128 * i + 256, :]
    big = jnp.dot(jnp.concatenate(band, axis=0), hi, preferred_element_type=f32)
    small = jnp.dot(band[0], lo, preferred_element_type=f32)
    return big[:128] + (big[128:] + small)


def share_kernel(
    index_hbm, taps_hbm, rec_hbm, exch_ref, index_ref, taps_ref, rec_ref, hi_ref, lo_ref, ext_ref, sems, *, pair
):
    rows, width = rec_ref.shape
    sources = index_ref.shape[0]
    step = rows // FETCHES
    fetches = [pltpu.make_async_copy(taps_hbm, taps_ref, sems.at[FETCHES + 1])]
    for i in range(FETCHES):
        part = pl.ds(i * step, step)
        fetches.append(pltpu.make_async_copy(rec_hbm.at[part, :], rec_ref.at[part, :], sems.at[i]))
    fetches.append(pltpu.make_async_copy(index_hbm, index_ref, sems.at[FETCHES]))
    for fetch in fetches:
        fetch.start()
    clear_edges((hi_ref, lo_ref), rows)
    fetches[0].wait()
    band = band_halves(taps_ref, 0)
    for i in range(FETCHES):
        fetches[1 + i].wait()
        split_rows(rec_ref[i * step : (i + 1) * step, :], hi_ref, lo_ref, 64 + i * step)
    fetches[1 + FETCHES].wait()
    for i in range(ext_ref.shape[0] // 128):
        ext_ref[128 * i : 128 * i + 128, :] = band_product(band, hi_ref, lo_ref, i)
    first = lax.axis_index("sec") * rows - HALO
    for s in range(sources):
        row = index_ref[s] - first
        inside = jnp.logical_and(row >= 0, row < rows + 2 * HALO)
        at = jnp.where(inside, row, 0)
        exch_ref[s : s + 1, :] = jnp.where(inside, ext_ref[pl.ds(at, 1), :], 0.0)
    down = ext_ref[:HALO, :]
    up = ext_ref[HALO + rows : 2 * HALO + rows, :]
    if pair:
        exch_ref[sources:, :] = jnp.where(lax.axis_index("sec") == 0, up, down)
    else:
        exch_ref[sources : sources + HALO, :] = down
        exch_ref[sources + HALO :, :] = up


def share(record, fir_taps, source_index, pair):
    rows, width = record.shape
    sources = source_index.shape[0]
    tiles = -(-(rows + 64) // 128)
    return pl.pallas_call(
        functools.partial(share_kernel, pair=pair),
        out_shape=jax.ShapeDtypeStruct((sources + HALO * (1 if pair else 2), width), f32),
        in_specs=[pl.BlockSpec(memory_space=pltpu.HBM)] * 3,
        scratch_shapes=[
            pltpu.SMEM(source_index.shape, jnp.int32),
            pltpu.SMEM(fir_taps.shape, f32),
            pltpu.VMEM((rows, width), f32),
            pltpu.VMEM((128 * (tiles + 1), width), bf16),
            pltpu.VMEM((128 * (tiles + 1), width), bf16),
            pltpu.VMEM((128 * tiles, width), f32),
            pltpu.SemaphoreType.DMA((FETCHES + 2,)),
        ],
        compiler_params=pltpu.CompilerParams(vmem_limit_bytes=VMEM_ALL),
        cost_estimate=pl.CostEstimate(flops=2 * 3 * 128 * tiles * 256 * width, bytes_accessed=4 * rows * width, transcendentals=0),
    )(source_index, fir_taps, record)


def filter_kernel(taps_ref, rec_ref, filt_ref, hi_ref, lo_ref):
    rows = rec_ref.shape[0]
    clear_edges((hi_ref, lo_ref), rows)
    band = band_halves(taps_ref, HALO)
    split_rows(rec_ref[...], hi_ref, lo_ref, 64)
    for i in range(rows // 128):
        filt_ref[128 * i : 128 * i + 128, :] = band_product(band, hi_ref, lo_ref, i)


def filter_rows(record, fir_taps):
    rows, width = record.shape
    return pl.pallas_call(
        filter_kernel,
        out_shape=jax.ShapeDtypeStruct((rows, width), f32),
        in_specs=[pl.BlockSpec(memory_space=pltpu.SMEM), pl.BlockSpec(memory_space=pltpu.VMEM)],
        scratch_shapes=[pltpu.VMEM((rows + 128, width), bf16), pltpu.VMEM((rows + 128, width), bf16)],
        compiler_params=pltpu.CompilerParams(vmem_limit_bytes=24 * 1024 * 1024),
        cost_estimate=pl.CostEstimate(flops=2 * 3 * rows * 256 * width, bytes_accessed=8 * rows * width, transcendentals=0),
    )(fir_taps, record)


def pack_kernel(filt_ref, *refs, count, sources, pair):
    rows = filt_ref.shape[0]
    out_ref = refs[-1]
    if pair:
        here_ref, there_ref = refs[:2]
        pilots = here_ref[:sources, :] + there_ref[:sources, :]
        edge = there_ref[sources:, :]
        second = lax.axis_index("sec") == 1
        low = jnp.where(second, edge, 0.0)
        high = jnp.where(second, 0.0, edge)
    else:
        pilots, low, high = (ref[...] for ref in refs[:3])
    pilots = pilots.astype(bf16)
    for d in range(out_ref.shape[0]):
        out_ref[d, :sources, :] = pilots
        lo, hi = d * count, (d + 1) * count
        part = filt_ref[lo:hi, :]
        if lo < HALO:
            n = min(hi, HALO) - lo
            add = low[lo : lo + n, :]
            part = jnp.concatenate([part[:n] + add, part[n:]], axis=0) if n < count else part + add
        if hi > rows - HALO:
            start = max(lo, rows - HALO)
            add = high[start - (rows - HALO) : hi - (rows - HALO), :]
            n = hi - start
            part = jnp.concatenate([part[: count - n], part[count - n :] + add], axis=0) if n < count else part + add
        out_ref[d, sources:, :] = part.astype(bf16)


def pack(filt, others, devices, sources, pair):
    rows, width = filt.shape
    count = rows // devices
    return pl.pallas_call(
        functools.partial(pack_kernel, count=count, sources=sources, pair=pair),
        out_shape=jax.ShapeDtypeStruct((devices, sources + count, width), bf16),
        compiler_params=pltpu.CompilerParams(vmem_limit_bytes=24 * 1024 * 1024),
    )(filt, *others)


def corr_kernel(x_ref, o_ref, lo_ref, v_ref, z_ref, acc_ref, *, kc, count):
    wins, _, win = x_ref.shape
    T=wins*win
    KT=T+256
    nt=T//128
    per=win//128
    esum=jnp.zeros((16,128),f32)
    usum=jnp.zeros((count,128),f32)
    zlo=jnp.zeros((16,256),bf16)
    lo_ref[:,:256]=zlo
    lo_ref[:,256+T:]=zlo[:,:128]
    v_ref[:,:128]=zlo[:,:128]
    v_ref[:,256+T:]=zlo[:,:128]
    lane8=lax.broadcasted_iota(jnp.int32,(8,128),1)
    def him(a,b):
        return jnp.concatenate([a,jnp.where(lane8<112,pltpu.roll(a,112,1),pltpu.roll(b,112,1))],axis=0).astype(bf16)
    z8=jnp.zeros((8,128),f32)
    prev=z8
    for k in range(nt):
        w,q=divmod(k,per); s=slice(q*128,q*128+128)
        p=x_ref[w,0:16,s].astype(f32)
        u=x_ref[w,16:16+count,s].astype(f32)
        esum=esum+p*p; usum=usum+u*u
        lo_ref[:,256+128*k:384+128*k]=x_ref[w,16:32,s]
        v_ref[:,128+128*k:256+128*k]=him(prev,u[16:])
        prev=u[16:]
    v_ref[:,128+T:256+T]=him(prev,z8)
    lane=lax.broadcasted_iota(jnp.int32,(16,128),1)
    zp=jnp.zeros((16,128),bf16)
    for q in range(4): z_ref[q,:,:512]=jnp.zeros((16,512),bf16)
    def ptile(k):
        if k>=nt: return zp
        w,q=divmod(k,per)
        return x_ref[w,0:16,q*128:q*128+128]
    state=[[zp]*4,[zp]*4]
    def zbuild(k):
        t=ptile(k)
        rolls=[t]+[pltpu.roll(t,32*q,1) for q in (1,2,3)]
        S=[t]+[jnp.where(lane<32*q,state[0][q],rolls[q]) for q in (1,2,3)]
        for q in range(4): z_ref[q,:,512+128*k:640+128*k]=S[q]
        state[0]=rolls; state[1]=S
    steps=-(-KT//kc)
    def chunk(t0,first):
        X=lo_ref[:,pl.ds(t0,kc+128)]
        V=v_ref[:,pl.ds(t0,kc+128)]
        w=kc+128
        rows=[(pltpu.roll(X,w-j,1) if j else X)[:,:kc] for j in range(G+1)]
        rows+=[(pltpu.roll(V,w-j,1) if j else V)[:,:kc] for j in range(G//2)]
        rows.append(pltpu.roll(V,w-16,1)[:,:kc])
        plate=jnp.concatenate(rows,axis=0)
        rhs=jnp.concatenate([z_ref[g%4,:,pl.ds(t0+512-128*(g//4),kc)] for g in range(16)],axis=0)
        d=lax.dot_general(plate,rhs,(((1,),(1,)),((),())),preferred_element_type=f32)
        for a in range(2):
            if first: acc_ref[a]=d[:,128*a:128*a+128]
            else: acc_ref[a]+=d[:,128*a:128*a+128]
    for i in range(steps):
        for k in range(i*kc//128,(i+1)*kc//128): zbuild(k)
        chunk(i*kc,i==0)
    es=lax.rsqrt(jnp.sum(esum,axis=1,keepdims=True)/T+EPS)
    ue=lax.rsqrt(jnp.sum(usum,axis=1,keepdims=True)/T+EPS)/math.sqrt(T)
    esb=jnp.broadcast_to(es,(16,128))
    hi0=16*(G+1)
    def lags(h,c):
        if c<16: return acc_ref[h,pl.ds(c,32,stride=16),:]
        return jnp.concatenate([acc_ref[h,pl.ds(hi0+c-16,16,stride=16),:],acc_ref[h,pl.ds(hi0+c-8,16,stride=16),:]],axis=0)
    for quad in range(count//4):
        scl=[esb*jnp.broadcast_to(ue[4*quad+m:4*quad+m+1],(16,128)) for m in range(4)]
        for h in range(2):
            Y=jnp.concatenate([lags(h,4*quad+m) for m in range(4)],axis=0).T
            for b in range(2):
                for m in range(4):
                    o=None
                    for q in range(4):
                        v=Y[64*b+16*q:64*b+16*q+16,:]
                        sh=(32*(q-m))%128
                        v=pltpu.roll(v,sh,1) if sh else v
                        o=v if o is None else jnp.where(lane<32*q,o,v)
                    o_ref[4*quad+m,:,(2*h+b)*128:(2*h+b)*128+128]=o*scl[m]
    last=jnp.concatenate([acc_ref[1,512:528,:],acc_ref[1,hi0+264:hi0+272,:]],axis=0)
    last=jnp.concatenate([last*ue,jnp.zeros((104,128),f32)],axis=0).T[112:128]*es
    for c in range(count):
        v=pltpu.roll(last,128-c,1) if c else last
        o_ref[c,:,512:513]=v[:,0:1]
def correlate(x,kc=2816):
    wins,rows,win=x.shape
    count=rows-16
    T=wins*win
    out=pl.pallas_call(functools.partial(corr_kernel,kc=kc,count=count),
        out_shape=jax.ShapeDtypeStruct((count,16,NLAG),f32),
        scratch_shapes=[pltpu.VMEM((16,T+384),bf16),pltpu.VMEM((16,T+384),bf16),pltpu.VMEM((4,16,T+768),bf16),pltpu.VMEM((2,16*(3*G//2+2),128),f32)],
        compiler_params=pltpu.CompilerParams(vmem_limit_bytes=48*1024*1024),
    )(x)
    return out


def shards(record, fir_taps, source_index):
    sections = lax.axis_size("sec")
    pair = sections == 2
    sources = source_index.shape[0]
    exch = share(record, fir_taps, source_index, pair)
    filt = filter_rows(record, fir_taps)
    if pair:
        others = (exch, lax.ppermute(exch, "sec", [(0, 1), (1, 0)]))
    else:
        pilots = lax.psum(exch[:sources], "sec")
        up = [(i, i + 1) for i in range(sections - 1)]
        down = [(i + 1, i) for i in range(sections - 1)]
        high = lax.ppermute(exch[sources : sources + HALO], "sec", down)
        low = lax.ppermute(exch[sources + HALO :], "sec", up)
        others = (pilots, low, high)
    blocks = pack(filt, others, lax.axis_size("tm"), sources, pair)
    return correlate(lax.all_to_all(blocks, "tm", 0, 0, tiled=True))


def solution(mesh):
    in_specs = (P("sec", "tm"), P(), P())
    out_specs = P(("sec", "tm"), None, None)
    return jax.shard_map(shards, mesh=mesh, in_specs=in_specs, out_specs=out_specs, check_vma=False)
```

```python
import functools
import math

import jax
import jax.numpy as jnp
from jax import lax
from jax.experimental import pallas as pl
from jax.experimental.pallas import tpu as pltpu
from jax.sharding import PartitionSpec as P

f32 = jnp.float32
bf16 = jnp.bfloat16
HALF_LAG = 256
NLAG = 2 * HALF_LAG + 1
SCALE = 2.0**32
EPS = 1e-6 * SCALE * SCALE
G = 32
HALO = 32
HALF = 8
FETCHES = 3
VMEM_ALL = 64 * 1024 * 1024


def band_halves(taps_ref, shift):
    lane = lax.broadcasted_iota(jnp.int32, (8, 256), 1)
    base = jnp.zeros((8, 256), f32)
    for m in range(taps_ref.shape[0]):
        base = jnp.where(lane == m, taps_ref[m] * SCALE, base)
    tall = jnp.concatenate([base] * 16, axis=0)
    band = pltpu.roll(tall, shift, 1, stride=1, stride_axis=0)
    high = band.astype(bf16)
    return high, (band - high.astype(f32)).astype(bf16)


def clear_edges(refs, rows):
    for ref in refs:
        deep, width = ref.shape
        ref[:64, :] = jnp.zeros((64, width), bf16)
        ref[64 + rows :, :] = jnp.zeros((deep - 64 - rows, width), bf16)


def split_rows(rec, hi_ref, lo_ref, at):
    high = rec.astype(bf16)
    hi_ref[at : at + rec.shape[0], :] = high
    lo_ref[at : at + rec.shape[0], :] = (rec - high.astype(f32)).astype(bf16)


def band_product(band, hi_ref, lo_ref, i):
    hi = hi_ref[128 * i : 128 * i + 256, :]
    lo = lo_ref[128 * i : 128 * i + 256, :]
    big = jnp.dot(jnp.concatenate(band, axis=0), hi, preferred_element_type=f32)
    small = jnp.dot(band[0], lo, preferred_element_type=f32)
    return big[:128] + (big[128:] + small)


def share_kernel(
    index_hbm, taps_hbm, rec_hbm, exch_ref, index_ref, taps_ref, rec_ref, hi_ref, lo_ref, ext_ref, sems, *, pair
):
    rows, width = rec_ref.shape
    sources = index_ref.shape[0]
    step = rows // FETCHES
    fetches = [pltpu.make_async_copy(taps_hbm, taps_ref, sems.at[FETCHES + 1])]
    for i in range(FETCHES):
        part = pl.ds(i * step, step)
        fetches.append(pltpu.make_async_copy(rec_hbm.at[part, :], rec_ref.at[part, :], sems.at[i]))
    fetches.append(pltpu.make_async_copy(index_hbm, index_ref, sems.at[FETCHES]))
    for fetch in fetches:
        fetch.start()
    clear_edges((hi_ref, lo_ref), rows)
    fetches[0].wait()
    band = band_halves(taps_ref, 0)
    for i in range(FETCHES):
        fetches[1 + i].wait()
        split_rows(rec_ref[i * step : (i + 1) * step, :], hi_ref, lo_ref, 64 + i * step)
    fetches[1 + FETCHES].wait()
    for i in range(ext_ref.shape[0] // 128):
        ext_ref[128 * i : 128 * i + 128, :] = band_product(band, hi_ref, lo_ref, i)
    first = lax.axis_index("sec") * rows - HALO
    for s in range(sources):
        row = index_ref[s] - first
        inside = jnp.logical_and(row >= 0, row < rows + 2 * HALO)
        at = jnp.where(inside, row, 0)
        exch_ref[s : s + 1, :] = jnp.where(inside, ext_ref[pl.ds(at, 1), :], 0.0)
    down = ext_ref[:HALO, :]
    up = ext_ref[HALO + rows : 2 * HALO + rows, :]
    if pair:
        exch_ref[sources:, :] = jnp.where(lax.axis_index("sec") == 0, up, down)
    else:
        exch_ref[sources : sources + HALO, :] = down
        exch_ref[sources + HALO :, :] = up


def share(record, fir_taps, source_index, pair):
    rows, width = record.shape
    sources = source_index.shape[0]
    tiles = -(-(rows + 64) // 128)
    return pl.pallas_call(
        functools.partial(share_kernel, pair=pair),
        out_shape=jax.ShapeDtypeStruct((sources + HALO * (1 if pair else 2), width), f32),
        in_specs=[pl.BlockSpec(memory_space=pltpu.HBM)] * 3,
        scratch_shapes=[
            pltpu.SMEM(source_index.shape, jnp.int32),
            pltpu.SMEM(fir_taps.shape, f32),
            pltpu.VMEM((rows, width), f32),
            pltpu.VMEM((128 * (tiles + 1), width), bf16),
            pltpu.VMEM((128 * (tiles + 1), width), bf16),
            pltpu.VMEM((128 * tiles, width), f32),
            pltpu.SemaphoreType.DMA((FETCHES + 2,)),
        ],
        compiler_params=pltpu.CompilerParams(vmem_limit_bytes=VMEM_ALL),
        cost_estimate=pl.CostEstimate(flops=2 * 3 * 128 * tiles * 256 * width, bytes_accessed=4 * rows * width, transcendentals=0),
    )(source_index, fir_taps, record)


def filter_kernel(taps_ref, rec_ref, filt_ref, hi_ref, lo_ref):
    rows = rec_ref.shape[0]
    clear_edges((hi_ref, lo_ref), rows)
    band = band_halves(taps_ref, HALO)
    split_rows(rec_ref[...], hi_ref, lo_ref, 64)
    for i in range(rows // 128):
        filt_ref[128 * i : 128 * i + 128, :] = band_product(band, hi_ref, lo_ref, i)


def filter_rows(record, fir_taps):
    rows, width = record.shape
    return pl.pallas_call(
        filter_kernel,
        out_shape=jax.ShapeDtypeStruct((rows, width), f32),
        in_specs=[pl.BlockSpec(memory_space=pltpu.SMEM), pl.BlockSpec(memory_space=pltpu.VMEM)],
        scratch_shapes=[pltpu.VMEM((rows + 128, width), bf16), pltpu.VMEM((rows + 128, width), bf16)],
        compiler_params=pltpu.CompilerParams(vmem_limit_bytes=24 * 1024 * 1024),
        cost_estimate=pl.CostEstimate(flops=2 * 3 * rows * 256 * width, bytes_accessed=8 * rows * width, transcendentals=0),
    )(fir_taps, record)


def pack_kernel(filt_ref, *refs, count, sources, pair):
    rows = filt_ref.shape[0]
    out_ref = refs[-1]
    if pair:
        here_ref, there_ref = refs[:2]
        pilots = here_ref[:sources, :] + there_ref[:sources, :]
        edge = there_ref[sources:, :]
        second = lax.axis_index("sec") == 1
        low = jnp.where(second, edge, 0.0)
        high = jnp.where(second, 0.0, edge)
    else:
        pilots, low, high = (ref[...] for ref in refs[:3])
    for d in range(out_ref.shape[0]):
        own = pilots[HALF * (d % 2) : HALF * (d % 2) + HALF]
        lo, hi = d * count, (d + 1) * count
        part = filt_ref[lo:hi, :]
        if lo < HALO:
            n = min(hi, HALO) - lo
            add = low[lo : lo + n, :]
            part = jnp.concatenate([part[:n] + add, part[n:]], axis=0) if n < count else part + add
        if hi > rows - HALO:
            start = max(lo, rows - HALO)
            add = high[start - (rows - HALO) : hi - (rows - HALO), :]
            n = hi - start
            part = jnp.concatenate([part[: count - n], part[count - n :] + add], axis=0) if n < count else part + add
        out_ref[d] = jnp.concatenate([own, part], axis=0).astype(bf16)


def pack(filt, others, devices, sources, pair):
    rows, width = filt.shape
    count = rows // devices
    return pl.pallas_call(
        functools.partial(pack_kernel, count=count, sources=sources, pair=pair),
        out_shape=jax.ShapeDtypeStruct((devices, HALF + count, width), bf16),
        compiler_params=pltpu.CompilerParams(vmem_limit_bytes=24 * 1024 * 1024),
    )(filt, *others)


def corr_kernel(x_ref, other_ref, o_ref, p_ref, lo_ref, v_ref, z_ref, acc_ref, *, kc, count):
    wins, _, win = x_ref.shape
    T=wins*win
    KT=T+256
    nt=T//128
    per=win//128
    esum=jnp.zeros((16,128),f32)
    usum=jnp.zeros((count,128),f32)
    zlo=jnp.zeros((16,256),bf16)
    lo_ref[:,:256]=zlo
    lo_ref[:,256+T:]=zlo[:,:128]
    v_ref[:,:128]=zlo[:,:128]
    v_ref[:,256+T:]=zlo[:,:128]
    lane8=lax.broadcasted_iota(jnp.int32,(8,128),1)
    def him(a,b):
        return jnp.concatenate([a,jnp.where(lane8<112,pltpu.roll(a,112,1),pltpu.roll(b,112,1))],axis=0).astype(bf16)
    z8=jnp.zeros((8,128),f32)
    prev=z8
    for k in range(nt):
        w,q=divmod(k,per); s=slice(q*128,q*128+128)
        block=x_ref[w,:,s].astype(f32)
        p=jnp.concatenate([block[:HALF],other_ref[w,:,s].astype(f32)],axis=0)
        u=block[HALF:]
        esum=esum+p*p; usum=usum+u*u
        p_ref[:,128*k:128*k+128]=p.astype(bf16)
        lo_ref[:,256+128*k:384+128*k]=u[:16].astype(bf16)
        v_ref[:,128+128*k:256+128*k]=him(prev,u[16:])
        prev=u[16:]
    v_ref[:,128+T:256+T]=him(prev,z8)
    lane=lax.broadcasted_iota(jnp.int32,(16,128),1)
    zp=jnp.zeros((16,128),bf16)
    for q in range(4): z_ref[q,:,:512]=jnp.zeros((16,512),bf16)
    def ptile(k):
        if k>=nt: return zp
        return p_ref[:,128*k:128*k+128]
    state=[[zp]*4,[zp]*4]
    def zbuild(k):
        t=ptile(k)
        rolls=[t]+[pltpu.roll(t,32*q,1) for q in (1,2,3)]
        S=[t]+[jnp.where(lane<32*q,state[0][q],rolls[q]) for q in (1,2,3)]
        for q in range(4): z_ref[q,:,512+128*k:640+128*k]=S[q]
        state[0]=rolls; state[1]=S
    steps=-(-KT//kc)
    def chunk(t0,first):
        X=lo_ref[:,pl.ds(t0,kc+128)]
        V=v_ref[:,pl.ds(t0,kc+128)]
        w=kc+128
        rows=[(pltpu.roll(X,w-j,1) if j else X)[:,:kc] for j in range(G+1)]
        rows+=[(pltpu.roll(V,w-j,1) if j else V)[:,:kc] for j in range(G//2)]
        rows.append(pltpu.roll(V,w-16,1)[:,:kc])
        plate=jnp.concatenate(rows,axis=0)
        rhs=jnp.concatenate([z_ref[g%4,:,pl.ds(t0+512-128*(g//4),kc)] for g in range(16)],axis=0)
        d=lax.dot_general(plate,rhs,(((1,),(1,)),((),())),preferred_element_type=f32)
        for a in range(2):
            if first: acc_ref[a]=d[:,128*a:128*a+128]
            else: acc_ref[a]+=d[:,128*a:128*a+128]
    for i in range(steps):
        for k in range(i*kc//128,(i+1)*kc//128): zbuild(k)
        chunk(i*kc,i==0)
    es=lax.rsqrt(jnp.sum(esum,axis=1,keepdims=True)/T+EPS)
    ue=lax.rsqrt(jnp.sum(usum,axis=1,keepdims=True)/T+EPS)/math.sqrt(T)
    esb=jnp.broadcast_to(es,(16,128))
    hi0=16*(G+1)
    mine=pl.multiple_of(lax.axis_index("tm")%2*HALF,HALF)
    theirs=pl.multiple_of(HALF-mine,HALF)
    def put(c,at,v):
        o_ref[c,pl.ds(mine,HALF),at:at+v.shape[1]]=v[:HALF]
        o_ref[c,pl.ds(theirs,HALF),at:at+v.shape[1]]=v[HALF:]
    def lags(h,c):
        if c<16: return acc_ref[h,pl.ds(c,32,stride=16),:]
        return jnp.concatenate([acc_ref[h,pl.ds(hi0+c-16,16,stride=16),:],acc_ref[h,pl.ds(hi0+c-8,16,stride=16),:]],axis=0)
    for quad in range(count//4):
        scl=[esb*jnp.broadcast_to(ue[4*quad+m:4*quad+m+1],(16,128)) for m in range(4)]
        for h in range(2):
            Y=jnp.concatenate([lags(h,4*quad+m) for m in range(4)],axis=0).T
            for b in range(2):
                for m in range(4):
                    o=None
                    for q in range(4):
                        v=Y[64*b+16*q:64*b+16*q+16,:]
                        sh=(32*(q-m))%128
                        v=pltpu.roll(v,sh,1) if sh else v
                        o=v if o is None else jnp.where(lane<32*q,o,v)
                    put(4*quad+m,(2*h+b)*128,o*scl[m])
    last=jnp.concatenate([acc_ref[1,512:528,:],acc_ref[1,hi0+264:hi0+272,:]],axis=0)
    last=jnp.concatenate([last*ue,jnp.zeros((104,128),f32)],axis=0).T[112:128]*es
    for c in range(count):
        v=pltpu.roll(last,128-c,1) if c else last
        put(c,512,v[:,0:1])
def correlate(x,other,kc=2816):
    wins,rows,win=x.shape
    count=rows-HALF
    T=wins*win
    out=pl.pallas_call(functools.partial(corr_kernel,kc=kc,count=count),
        out_shape=jax.ShapeDtypeStruct((count,16,NLAG),f32),
        scratch_shapes=[pltpu.VMEM((16,T),bf16),pltpu.VMEM((16,T+384),bf16),pltpu.VMEM((16,T+384),bf16),pltpu.VMEM((4,16,T+768),bf16),pltpu.VMEM((2,16*(3*G//2+2),128),f32)],
        compiler_params=pltpu.CompilerParams(vmem_limit_bytes=48*1024*1024),
    )(x,other)
    return out


def shards(record, fir_taps, source_index):
    sections = lax.axis_size("sec")
    pair = sections == 2
    sources = source_index.shape[0]
    exch = share(record, fir_taps, source_index, pair)
    filt = filter_rows(record, fir_taps)
    if pair:
        others = (exch, lax.ppermute(exch, "sec", [(0, 1), (1, 0)]))
    else:
        pilots = lax.psum(exch[:sources], "sec")
        up = [(i, i + 1) for i in range(sections - 1)]
        down = [(i + 1, i) for i in range(sections - 1)]
        high = lax.ppermute(exch[sources : sources + HALO], "sec", down)
        low = lax.ppermute(exch[sources + HALO :], "sec", up)
        others = (pilots, low, high)
    blocks = pack(filt, others, lax.axis_size("tm"), sources, pair)
    blocks = lax.all_to_all(blocks, "tm", 0, 0, tiled=True)
    swap = [(i, i ^ 1) for i in range(lax.axis_size("tm"))]
    other = lax.ppermute(blocks[:, :HALF], "tm", swap)
    return correlate(blocks, other)


def solution(mesh):
    in_specs = (P("sec", "tm"), P(), P())
    out_specs = P(("sec", "tm"), None, None)
    return jax.shard_map(shards, mesh=mesh, in_specs=in_specs, out_specs=out_specs, check_vma=False)
```

```python
import functools
import math

import jax
import jax.numpy as jnp
from jax import lax
from jax.experimental import pallas as pl
from jax.experimental.pallas import tpu as pltpu
from jax.sharding import PartitionSpec as P

f32 = jnp.float32
bf16 = jnp.bfloat16
HALF_LAG = 256
NLAG = 2 * HALF_LAG + 1
SCALE = 2.0**32
EPS = 1e-6 * SCALE * SCALE
G = 32
HALO = 32
HALF = 8
SENT = 4
FETCHES = 3


def band_halves(taps_ref, shift):
    lane = lax.broadcasted_iota(jnp.int32, (8, 256), 1)
    base = jnp.zeros((8, 256), f32)
    for m in range(taps_ref.shape[0]):
        base = jnp.where(lane == m, taps_ref[m] * SCALE, base)
    tall = jnp.concatenate([base] * 16, axis=0)
    band = pltpu.roll(tall, shift, 1, stride=1, stride_axis=0)
    high = band.astype(bf16)
    return high, (band - high.astype(f32)).astype(bf16)


def clear_edges(refs, rows):
    for ref in refs:
        deep, width = ref.shape
        ref[:64, :] = jnp.zeros((64, width), bf16)
        ref[64 + rows :, :] = jnp.zeros((deep - 64 - rows, width), bf16)


def split_rows(rec, hi_ref, lo_ref, at):
    high = rec.astype(bf16)
    hi_ref[at : at + rec.shape[0], :] = high
    lo_ref[at : at + rec.shape[0], :] = (rec - high.astype(f32)).astype(bf16)


def band_product(band, hi_ref, lo_ref, i):
    hi = hi_ref[128 * i : 128 * i + 256, :]
    lo = lo_ref[128 * i : 128 * i + 256, :]
    big = jnp.dot(jnp.concatenate(band, axis=0), hi, preferred_element_type=f32)
    small = jnp.dot(band[0], lo, preferred_element_type=f32)
    return big[:128] + (big[128:] + small)


def share_kernel(
    index_hbm, taps_hbm, rec_hbm, exch_ref, index_ref, taps_ref, rec_ref, hi_ref, lo_ref, ext_ref, sems, *, pair
):
    rows, width = rec_ref.shape
    sources = index_ref.shape[0]
    step = rows // FETCHES
    fetches = [pltpu.make_async_copy(taps_hbm, taps_ref, sems.at[FETCHES + 1])]
    for i in range(FETCHES):
        part = pl.ds(i * step, step)
        fetches.append(pltpu.make_async_copy(rec_hbm.at[part, :], rec_ref.at[part, :], sems.at[i]))
    fetches.append(pltpu.make_async_copy(index_hbm, index_ref, sems.at[FETCHES]))
    for fetch in fetches:
        fetch.start()
    clear_edges((hi_ref, lo_ref), rows)
    fetches[0].wait()
    band = band_halves(taps_ref, 0)
    for i in range(FETCHES):
        fetches[1 + i].wait()
        split_rows(rec_ref[i * step : (i + 1) * step, :], hi_ref, lo_ref, 64 + i * step)
    fetches[1 + FETCHES].wait()
    for i in range(ext_ref.shape[0] // 128):
        ext_ref[128 * i : 128 * i + 128, :] = band_product(band, hi_ref, lo_ref, i)
    first = lax.axis_index("sec") * rows - HALO
    for s in range(sources):
        row = index_ref[s] - first
        inside = jnp.logical_and(row >= 0, row < rows + 2 * HALO)
        at = jnp.where(inside, row, 0)
        exch_ref[s : s + 1, :] = jnp.where(inside, ext_ref[pl.ds(at, 1), :], 0.0)
    down = ext_ref[:HALO, :]
    up = ext_ref[HALO + rows : 2 * HALO + rows, :]
    if pair:
        exch_ref[sources:, :] = jnp.where(lax.axis_index("sec") == 0, up, down)
    else:
        exch_ref[sources : sources + HALO, :] = down
        exch_ref[sources + HALO :, :] = up


def share(record, fir_taps, source_index, pair):
    rows, width = record.shape
    sources = source_index.shape[0]
    tiles = -(-(rows + 64) // 128)
    return pl.pallas_call(
        functools.partial(share_kernel, pair=pair),
        out_shape=jax.ShapeDtypeStruct((sources + HALO * (1 if pair else 2), width), f32),
        in_specs=[pl.BlockSpec(memory_space=pltpu.HBM)] * 3,
        scratch_shapes=[
            pltpu.SMEM(source_index.shape, jnp.int32),
            pltpu.SMEM(fir_taps.shape, f32),
            pltpu.VMEM((rows, width), f32),
            pltpu.VMEM((128 * (tiles + 1), width), bf16),
            pltpu.VMEM((128 * (tiles + 1), width), bf16),
            pltpu.VMEM((128 * tiles, width), f32),
            pltpu.SemaphoreType.DMA((FETCHES + 2,)),
        ],
        compiler_params=pltpu.CompilerParams(vmem_limit_bytes=24*1024*1024),
        cost_estimate=pl.CostEstimate(flops=2 * 3 * 128 * tiles * 256 * width, bytes_accessed=4 * rows * width, transcendentals=0),
    )(source_index, fir_taps, record)


def filter_kernel(taps_ref, rec_ref, filt_ref, hi_ref, lo_ref):
    rows = rec_ref.shape[0]
    clear_edges((hi_ref, lo_ref), rows)
    band = band_halves(taps_ref, HALO)
    split_rows(rec_ref[...], hi_ref, lo_ref, 64)
    for i in range(rows // 128):
        filt_ref[128 * i : 128 * i + 128, :] = band_product(band, hi_ref, lo_ref, i)


def filter_rows(record, fir_taps):
    rows, width = record.shape
    return pl.pallas_call(
        filter_kernel,
        out_shape=jax.ShapeDtypeStruct((rows, width), f32),
        in_specs=[pl.BlockSpec(memory_space=pltpu.SMEM), pl.BlockSpec(memory_space=pltpu.VMEM)],
        scratch_shapes=[pltpu.VMEM((rows + 128, width), bf16), pltpu.VMEM((rows + 128, width), bf16)],
        compiler_params=pltpu.CompilerParams(vmem_limit_bytes=24 * 1024 * 1024),
        cost_estimate=pl.CostEstimate(flops=2 * 3 * rows * 256 * width, bytes_accessed=8 * rows * width, transcendentals=0),
    )(fir_taps, record)


def pack_kernel(filt_ref, *refs, count, sources, pair):
    rows = filt_ref.shape[0]
    out_ref = refs[-1]
    if pair:
        here_ref, there_ref = refs[:2]
        pilots = here_ref[:sources, :] + there_ref[:sources, :]
        edge = there_ref[sources:, :]
        second = lax.axis_index("sec") == 1
        low = jnp.where(second, edge, 0.0)
        high = jnp.where(second, 0.0, edge)
    else:
        pilots, low, high = (ref[...] for ref in refs[:3])
    for d in range(out_ref.shape[0]):
        own = pilots[HALF * (d % 2) : HALF * (d % 2) + HALF]
        lo, hi = d * count, (d + 1) * count
        part = filt_ref[lo:hi, :]
        if lo < HALO:
            n = min(hi, HALO) - lo
            add = low[lo : lo + n, :]
            part = jnp.concatenate([part[:n] + add, part[n:]], axis=0) if n < count else part + add
        if hi > rows - HALO:
            start = max(lo, rows - HALO)
            add = high[start - (rows - HALO) : hi - (rows - HALO), :]
            n = hi - start
            part = jnp.concatenate([part[: count - n], part[count - n :] + add], axis=0) if n < count else part + add
        out_ref[d] = jnp.concatenate([own, part], axis=0).astype(bf16)


def pack(filt, others, devices, sources, pair):
    rows, width = filt.shape
    count = rows // devices
    return pl.pallas_call(
        functools.partial(pack_kernel, count=count, sources=sources, pair=pair),
        out_shape=jax.ShapeDtypeStruct((devices, HALF + count, width), bf16),
        compiler_params=pltpu.CompilerParams(vmem_limit_bytes=24 * 1024 * 1024),
    )(filt, *others)


def corr_kernel(x_ref, other_ref, out_hbm, o_ref, sems, p_ref, lo_ref, v_ref, z_ref, acc_ref, *, kc, count):
    wins, _, win = x_ref.shape
    T=wins*win
    KT=T+256
    nt=T//128
    per=win//128
    esum=jnp.zeros((16,128),f32)
    usum=jnp.zeros((count,128),f32)
    zlo=jnp.zeros((16,256),bf16)
    lo_ref[:,:256]=zlo
    lo_ref[:,256+T:]=zlo[:,:128]
    v_ref[:,:128]=zlo[:,:128]
    v_ref[:,256+T:]=zlo[:,:128]
    lane8=lax.broadcasted_iota(jnp.int32,(8,128),1)
    def him(a,b):
        return jnp.concatenate([a,jnp.where(lane8<112,pltpu.roll(a,112,1),pltpu.roll(b,112,1))],axis=0).astype(bf16)
    z8=jnp.zeros((8,128),f32)
    prev=z8
    for k in range(nt):
        w,q=divmod(k,per); s=slice(q*128,q*128+128)
        block=x_ref[w,:,s].astype(f32)
        p=jnp.concatenate([block[:HALF],other_ref[w,:,s].astype(f32)],axis=0)
        u=block[HALF:]
        esum=esum+p*p; usum=usum+u*u
        p_ref[:,128*k:128*k+128]=p.astype(bf16)
        lo_ref[:,256+128*k:384+128*k]=u[:16].astype(bf16)
        v_ref[:,128+128*k:256+128*k]=him(prev,u[16:])
        prev=u[16:]
    v_ref[:,128+T:256+T]=him(prev,z8)
    lane=lax.broadcasted_iota(jnp.int32,(16,128),1)
    zp=jnp.zeros((16,128),bf16)
    for q in range(4): z_ref[q,:,:512]=jnp.zeros((16,512),bf16)
    def ptile(k):
        if k>=nt: return zp
        return p_ref[:,128*k:128*k+128]
    state=[[zp]*4,[zp]*4]
    def zbuild(k):
        t=ptile(k)
        rolls=[t]+[pltpu.roll(t,32*q,1) for q in (1,2,3)]
        S=[t]+[jnp.where(lane<32*q,state[0][q],rolls[q]) for q in (1,2,3)]
        for q in range(4): z_ref[q,:,512+128*k:640+128*k]=S[q]
        state[0]=rolls; state[1]=S
    steps=-(-KT//kc)
    def chunk(t0,first):
        X=lo_ref[:,pl.ds(t0,kc+128)]
        V=v_ref[:,pl.ds(t0,kc+128)]
        w=kc+128
        rows=[(pltpu.roll(X,w-j,1) if j else X)[:,:kc] for j in range(G+1)]
        rows+=[(pltpu.roll(V,w-j,1) if j else V)[:,:kc] for j in range(G//2)]
        rows.append(pltpu.roll(V,w-16,1)[:,:kc])
        plate=jnp.concatenate(rows,axis=0)
        rhs=jnp.concatenate([z_ref[q,:,pl.ds(t0+512-128*a,kc)] for q in range(4) for a in range(4)],axis=0)
        d=lax.dot_general(plate,rhs,(((1,),(1,)),((),())),preferred_element_type=f32)
        for a in range(2):
            if first: acc_ref[a]=d[:,128*a:128*a+128]
            else: acc_ref[a]+=d[:,128*a:128*a+128]
    for i in range(steps):
        for k in range(i*kc//128,(i+1)*kc//128): zbuild(k)
        chunk(i*kc,i==0)
    es=lax.rsqrt(jnp.sum(esum,axis=1,keepdims=True)/T+EPS)
    ue=lax.rsqrt(jnp.sum(usum,axis=1,keepdims=True)/T+EPS)/math.sqrt(T)
    esb=jnp.broadcast_to(es,(16,128))
    hi0=16*(G+1)
    mine=pl.multiple_of(lax.axis_index("tm")%2*HALF,HALF)
    theirs=pl.multiple_of(HALF-mine,HALF)
    def put(c,at,v):
        o_ref[c,pl.ds(mine,HALF),at:at+v.shape[1]]=v[:HALF]
        o_ref[c,pl.ds(theirs,HALF),at:at+v.shape[1]]=v[HALF:]
    def lags(h,c):
        if c<16: return acc_ref[h,pl.ds(c,32,stride=16),:]
        return jnp.concatenate([acc_ref[h,pl.ds(hi0+c-16,16,stride=16),:],acc_ref[h,pl.ds(hi0+c-8,16,stride=16),:]],axis=0)
    last=jnp.concatenate([acc_ref[1,512:528,:],acc_ref[1,hi0+264:hi0+272,:]],axis=0)
    last=jnp.concatenate([last*ue,jnp.zeros((104,128),f32)],axis=0).T[112:128]*es
    for c in range(count):
        v=pltpu.roll(last,128-c,1) if c else last
        put(c,512,v[:,0:1])
    copies=[]
    wide=lax.broadcasted_iota(jnp.int32,(32,128),1)<64
    for c in range(0,count,2):
        parts=[]
        for h in range(2):
            even,odd=lags(h,c),lags(h,c+1)
            parts.append(jnp.where(wide,even,pltpu.roll(odd,64,1)))
            parts.append(jnp.where(wide,pltpu.roll(even,64,1),odd))
        turned=jnp.concatenate(parts,axis=0).T
        for m in range(2):
            scl=esb*jnp.broadcast_to(ue[c+m:c+m+1],(16,128))
            for a in range(4):
                put(c+m,128*a,turned[64*m+16*a:64*m+16*a+16,:]*scl)
        if (c+2)%SENT==0:
            group=pl.ds(c+2-SENT,SENT)
            copies.append(pltpu.make_async_copy(o_ref.at[group],out_hbm.at[group],sems.at[c//SENT]))
            copies[-1].start()
    for copy in copies:
        copy.wait()


def correlate(x,other,kc=2816):
    wins,rows,win=x.shape
    count=rows-HALF
    T=wins*win
    out=pl.pallas_call(functools.partial(corr_kernel,kc=kc,count=count),
        out_shape=jax.ShapeDtypeStruct((count,16,NLAG),f32),
        out_specs=pl.BlockSpec(memory_space=pltpu.HBM),
        scratch_shapes=[pltpu.VMEM((count,16,NLAG),f32),pltpu.SemaphoreType.DMA((count//SENT,)),pltpu.VMEM((16,T),bf16),pltpu.VMEM((16,T+384),bf16),pltpu.VMEM((16,T+384),bf16),pltpu.VMEM((4,16,T+768),bf16),pltpu.VMEM((2,16*(3*G//2+2),128),f32)],
        compiler_params=pltpu.CompilerParams(vmem_limit_bytes=48*1024*1024),
    )(x,other)
    return out


def shards(record, fir_taps, source_index):
    sections = lax.axis_size("sec")
    pair = sections == 2
    sources = source_index.shape[0]
    hbm = [pltpu.with_memory_space_constraint(x, pltpu.HBM) for x in (record, fir_taps, source_index)]
    exch = share(*hbm, pair)
    filt = filter_rows(record, fir_taps)
    if pair:
        others = (exch, lax.ppermute(exch, "sec", [(0, 1), (1, 0)]))
    else:
        pilots = lax.psum(exch[:sources], "sec")
        up = [(i, i + 1) for i in range(sections - 1)]
        down = [(i + 1, i) for i in range(sections - 1)]
        high = lax.ppermute(exch[sources : sources + HALO], "sec", down)
        low = lax.ppermute(exch[sources + HALO :], "sec", up)
        others = (pilots, low, high)
    blocks = pack(filt, others, lax.axis_size("tm"), sources, pair)
    blocks = lax.all_to_all(blocks, "tm", 0, 0, tiled=True)
    swap = [(i, i ^ 1) for i in range(lax.axis_size("tm"))]
    other = lax.ppermute(blocks[:, :HALF], "tm", swap)
    return correlate(blocks, other)


def solution(mesh):
    in_specs = (P("sec", "tm"), P(), P())
    out_specs = P(("sec", "tm"), None, None)
    return jax.shard_map(shards, mesh=mesh, in_specs=in_specs, out_specs=out_specs, check_vma=False)
```

```python
import functools
import math

import jax
import jax.numpy as jnp
from jax import lax
from jax.experimental import pallas as pl
from jax.experimental.pallas import tpu as pltpu
from jax.sharding import PartitionSpec as P

f32 = jnp.float32
bf16 = jnp.bfloat16
HALF_LAG = 256
NLAG = 2 * HALF_LAG + 1
SCALE = 2.0**32
EPS = 1e-6 * SCALE * SCALE
G = 32
HALO = 32
HALF = 8
SENT = 4
FETCHES = 3


def band_halves(taps_ref, shift):
    lane = lax.broadcasted_iota(jnp.int32, (8, 256), 1)
    base = jnp.zeros((8, 256), f32)
    for m in range(taps_ref.shape[0]):
        base = jnp.where(lane == m, taps_ref[m] * SCALE, base)
    tall = jnp.concatenate([base] * 16, axis=0)
    band = pltpu.roll(tall, shift, 1, stride=1, stride_axis=0)
    high = band.astype(bf16)
    return high, (band - high.astype(f32)).astype(bf16)


def clear_edges(refs, rows):
    for ref in refs:
        deep, width = ref.shape
        ref[:64, :] = jnp.zeros((64, width), bf16)
        ref[64 + rows :, :] = jnp.zeros((deep - 64 - rows, width), bf16)


def split_rows(rec, hi_ref, lo_ref, at):
    high = rec.astype(bf16)
    hi_ref[at : at + rec.shape[0], :] = high
    lo_ref[at : at + rec.shape[0], :] = (rec - high.astype(f32)).astype(bf16)


def band_product(band, hi_ref, lo_ref, i):
    hi = hi_ref[128 * i : 128 * i + 256, :]
    lo = lo_ref[128 * i : 128 * i + 256, :]
    big = jnp.dot(jnp.concatenate(band, axis=0), hi, preferred_element_type=f32)
    small = jnp.dot(band[0], lo, preferred_element_type=f32)
    return big[:128] + (big[128:] + small)


def share_kernel(index_hbm, taps_hbm, rec_hbm, exch_ref, index_ref, taps_ref, rec_ref, sems, *, pair):
    rows, width = rec_ref.shape
    sources = index_ref.shape[0]
    taps = taps_ref.shape[0]
    step = rows // FETCHES
    fetches = [
        pltpu.make_async_copy(taps_hbm, taps_ref, sems.at[FETCHES + 1]),
        pltpu.make_async_copy(index_hbm, index_ref, sems.at[FETCHES]),
    ]
    for i in range(FETCHES):
        part = pl.ds(i * step, step)
        fetches.append(pltpu.make_async_copy(rec_hbm.at[part, :], rec_ref.at[part, :], sems.at[i]))
    for fetch in fetches:
        fetch.start()
    fetches[1].wait()
    first = lax.axis_index("sec") * rows + HALO
    at = lax.broadcasted_iota(jnp.int32, (sources, rows), 0)
    tap = jnp.zeros((sources, rows), jnp.int32)
    for s in range(sources):
        tap = jnp.where(at == s, index_ref[s] - first, tap)
    tap = lax.broadcasted_iota(jnp.int32, (sources, rows), 1) - tap
    ring = rows + 128
    lane = lax.broadcasted_iota(jnp.int32, (8, ring), 1)
    base = jnp.zeros((8, ring), f32)
    pick = jnp.zeros((sources, rows), f32)
    fetches[0].wait()
    for m in range(taps):
        value = taps_ref[m] * SCALE
        base = jnp.where(lane == m, value, base)
        pick = jnp.where(tap == m, value, pick)
    tall = jnp.concatenate([base] * (HALO // 8), axis=0)
    down = pltpu.roll(tall, ring - 64, 1, stride=1, stride_axis=0)[:, :rows]
    up = pltpu.roll(tall, rows - HALO, 1, stride=1, stride_axis=0)[:, :rows]
    edges = [jnp.where(lax.axis_index("sec") == 0, up, down)] if pair else [down, up]
    pick = jnp.concatenate([pick] + edges, axis=0)
    count = pick.shape[0]
    pick_hi = pick.astype(bf16)
    both = jnp.concatenate([pick_hi, (pick - pick_hi.astype(f32)).astype(bf16)], axis=0)
    total = jnp.zeros((count, width), f32)
    for i in range(FETCHES):
        fetches[2 + i].wait()
        part = slice(i * step, (i + 1) * step)
        rec = rec_ref[part, :]
        rec_hi = rec.astype(bf16)
        rec_lo = (rec - rec_hi.astype(f32)).astype(bf16)
        big = jnp.dot(both[:, part], rec_hi, preferred_element_type=f32)
        small = jnp.dot(pick_hi[:, part], rec_lo, preferred_element_type=f32)
        total = total + (big[:count] + (big[count:] + small))
    exch_ref[...] = total


def share(record, fir_taps, source_index, pair):
    rows, width = record.shape
    sources = source_index.shape[0]
    count = sources + HALO * (1 if pair else 2)
    return pl.pallas_call(
        functools.partial(share_kernel, pair=pair),
        out_shape=jax.ShapeDtypeStruct((count, width), f32),
        in_specs=[pl.BlockSpec(memory_space=pltpu.HBM)] * 3,
        scratch_shapes=[
            pltpu.SMEM(source_index.shape, jnp.int32),
            pltpu.SMEM(fir_taps.shape, f32),
            pltpu.VMEM((rows, width), f32),
            pltpu.SemaphoreType.DMA((FETCHES + 2,)),
        ],
        compiler_params=pltpu.CompilerParams(vmem_limit_bytes=24 * 1024 * 1024),
        cost_estimate=pl.CostEstimate(flops=6 * count * rows * width, bytes_accessed=4 * rows * width, transcendentals=0),
    )(source_index, fir_taps, record)


def filter_kernel(taps_ref, rec_ref, filt_ref, hi_ref, lo_ref):
    rows = rec_ref.shape[0]
    clear_edges((hi_ref, lo_ref), rows)
    band = band_halves(taps_ref, HALO)
    split_rows(rec_ref[...], hi_ref, lo_ref, 64)
    for i in range(rows // 128):
        filt_ref[128 * i : 128 * i + 128, :] = band_product(band, hi_ref, lo_ref, i)


def filter_rows(record, fir_taps):
    rows, width = record.shape
    return pl.pallas_call(
        filter_kernel,
        out_shape=jax.ShapeDtypeStruct((rows, width), f32),
        in_specs=[pl.BlockSpec(memory_space=pltpu.SMEM), pl.BlockSpec(memory_space=pltpu.VMEM)],
        scratch_shapes=[pltpu.VMEM((rows + 128, width), bf16), pltpu.VMEM((rows + 128, width), bf16)],
        compiler_params=pltpu.CompilerParams(vmem_limit_bytes=24 * 1024 * 1024),
        cost_estimate=pl.CostEstimate(flops=2 * 3 * rows * 256 * width, bytes_accessed=8 * rows * width, transcendentals=0),
    )(fir_taps, record)


def pack_kernel(filt_ref, *refs, count, sources, pair):
    rows = filt_ref.shape[0]
    out_ref = refs[-1]
    if pair:
        here_ref, there_ref = refs[:2]
        pilots = here_ref[:sources, :] + there_ref[:sources, :]
        edge = there_ref[sources:, :]
        second = lax.axis_index("sec") == 1
        low = jnp.where(second, edge, 0.0)
        high = jnp.where(second, 0.0, edge)
    else:
        pilots, low, high = (ref[...] for ref in refs[:3])
    for d in range(out_ref.shape[0]):
        own = pilots[HALF * (d % 2) : HALF * (d % 2) + HALF]
        lo, hi = d * count, (d + 1) * count
        part = filt_ref[lo:hi, :]
        if lo < HALO:
            n = min(hi, HALO) - lo
            add = low[lo : lo + n, :]
            part = jnp.concatenate([part[:n] + add, part[n:]], axis=0) if n < count else part + add
        if hi > rows - HALO:
            start = max(lo, rows - HALO)
            add = high[start - (rows - HALO) : hi - (rows - HALO), :]
            n = hi - start
            part = jnp.concatenate([part[: count - n], part[count - n :] + add], axis=0) if n < count else part + add
        out_ref[d] = jnp.concatenate([own, part], axis=0).astype(bf16)


def pack(filt, others, devices, sources, pair):
    rows, width = filt.shape
    count = rows // devices
    return pl.pallas_call(
        functools.partial(pack_kernel, count=count, sources=sources, pair=pair),
        out_shape=jax.ShapeDtypeStruct((devices, HALF + count, width), bf16),
        compiler_params=pltpu.CompilerParams(vmem_limit_bytes=24 * 1024 * 1024),
    )(filt, *others)


def corr_kernel(x_ref, other_ref, out_hbm, o_ref, sems, p_ref, lo_ref, v_ref, z_ref, acc_ref, *, kc, count):
    wins, _, win = x_ref.shape
    T=wins*win
    KT=T+256
    nt=T//128
    per=win//128
    esum=jnp.zeros((16,128),f32)
    usum=jnp.zeros((count,128),f32)
    zlo=jnp.zeros((16,256),bf16)
    lo_ref[:,:256]=zlo
    lo_ref[:,256+T:]=zlo[:,:128]
    v_ref[:,:128]=zlo[:,:128]
    v_ref[:,256+T:]=zlo[:,:128]
    lane8=lax.broadcasted_iota(jnp.int32,(8,128),1)
    def him(a,b):
        return jnp.concatenate([a,jnp.where(lane8<112,pltpu.roll(a,112,1),pltpu.roll(b,112,1))],axis=0).astype(bf16)
    z8=jnp.zeros((8,128),f32)
    prev=z8
    for k in range(nt):
        w,q=divmod(k,per); s=slice(q*128,q*128+128)
        block=x_ref[w,:,s].astype(f32)
        p=jnp.concatenate([block[:HALF],other_ref[w,:,s].astype(f32)],axis=0)
        u=block[HALF:]
        esum=esum+p*p; usum=usum+u*u
        p_ref[:,128*k:128*k+128]=p.astype(bf16)
        lo_ref[:,256+128*k:384+128*k]=u[:16].astype(bf16)
        v_ref[:,128+128*k:256+128*k]=him(prev,u[16:])
        prev=u[16:]
    v_ref[:,128+T:256+T]=him(prev,z8)
    lane=lax.broadcasted_iota(jnp.int32,(16,128),1)
    zp=jnp.zeros((16,128),bf16)
    for q in range(4): z_ref[q,:,:512]=jnp.zeros((16,512),bf16)
    def ptile(k):
        if k>=nt: return zp
        return p_ref[:,128*k:128*k+128]
    state=[[zp]*4,[zp]*4]
    def zbuild(k):
        t=ptile(k)
        rolls=[t]+[pltpu.roll(t,32*q,1) for q in (1,2,3)]
        S=[t]+[jnp.where(lane<32*q,state[0][q],rolls[q]) for q in (1,2,3)]
        for q in range(4): z_ref[q,:,512+128*k:640+128*k]=S[q]
        state[0]=rolls; state[1]=S
    steps=-(-KT//kc)
    def chunk(t0,first):
        X=lo_ref[:,pl.ds(t0,kc+128)]
        V=v_ref[:,pl.ds(t0,kc+128)]
        w=kc+128
        rows=[(pltpu.roll(X,w-j,1) if j else X)[:,:kc] for j in range(G+1)]
        rows+=[(pltpu.roll(V,w-j,1) if j else V)[:,:kc] for j in range(G//2)]
        rows.append(pltpu.roll(V,w-16,1)[:,:kc])
        plate=jnp.concatenate(rows,axis=0)
        rhs=jnp.concatenate([z_ref[q,:,pl.ds(t0+512-128*a,kc)] for q in range(4) for a in range(4)],axis=0)
        d=lax.dot_general(plate,rhs,(((1,),(1,)),((),())),preferred_element_type=f32)
        for a in range(2):
            if first: acc_ref[a]=d[:,128*a:128*a+128]
            else: acc_ref[a]+=d[:,128*a:128*a+128]
    for i in range(steps):
        for k in range(i*kc//128,(i+1)*kc//128): zbuild(k)
        chunk(i*kc,i==0)
    es=lax.rsqrt(jnp.sum(esum,axis=1,keepdims=True)/T+EPS)
    ue=lax.rsqrt(jnp.sum(usum,axis=1,keepdims=True)/T+EPS)/math.sqrt(T)
    esb=jnp.broadcast_to(es,(16,128))
    hi0=16*(G+1)
    mine=pl.multiple_of(lax.axis_index("tm")%2*HALF,HALF)
    theirs=pl.multiple_of(HALF-mine,HALF)
    def put(c,at,v):
        o_ref[c,pl.ds(mine,HALF),at:at+v.shape[1]]=v[:HALF]
        o_ref[c,pl.ds(theirs,HALF),at:at+v.shape[1]]=v[HALF:]
    def lags(h,c):
        if c<16: return acc_ref[h,pl.ds(c,32,stride=16),:]
        return jnp.concatenate([acc_ref[h,pl.ds(hi0+c-16,16,stride=16),:],acc_ref[h,pl.ds(hi0+c-8,16,stride=16),:]],axis=0)
    last=jnp.concatenate([acc_ref[1,512:528,:],acc_ref[1,hi0+264:hi0+272,:]],axis=0)
    last=jnp.concatenate([last*ue,jnp.zeros((104,128),f32)],axis=0).T[112:128]*es
    for c in range(count):
        v=pltpu.roll(last,128-c,1) if c else last
        put(c,512,v[:,0:1])
    copies=[]
    wide=lax.broadcasted_iota(jnp.int32,(32,128),1)<64
    for c in range(0,count,2):
        parts=[]
        for h in range(2):
            even,odd=lags(h,c),lags(h,c+1)
            parts.append(jnp.where(wide,even,pltpu.roll(odd,64,1)))
            parts.append(jnp.where(wide,pltpu.roll(even,64,1),odd))
        turned=jnp.concatenate(parts,axis=0).T
        for m in range(2):
            scl=esb*jnp.broadcast_to(ue[c+m:c+m+1],(16,128))
            for a in range(4):
                put(c+m,128*a,turned[64*m+16*a:64*m+16*a+16,:]*scl)
        if (c+2)%SENT==0:
            group=pl.ds(c+2-SENT,SENT)
            copies.append(pltpu.make_async_copy(o_ref.at[group],out_hbm.at[group],sems.at[c//SENT]))
            copies[-1].start()
    for copy in copies:
        copy.wait()


def correlate(x,other,kc=2816):
    wins,rows,win=x.shape
    count=rows-HALF
    T=wins*win
    out=pl.pallas_call(functools.partial(corr_kernel,kc=kc,count=count),
        out_shape=jax.ShapeDtypeStruct((count,16,NLAG),f32),
        out_specs=pl.BlockSpec(memory_space=pltpu.HBM),
        scratch_shapes=[pltpu.VMEM((count,16,NLAG),f32),pltpu.SemaphoreType.DMA((count//SENT,)),pltpu.VMEM((16,T),bf16),pltpu.VMEM((16,T+384),bf16),pltpu.VMEM((16,T+384),bf16),pltpu.VMEM((4,16,T+768),bf16),pltpu.VMEM((2,16*(3*G//2+2),128),f32)],
        compiler_params=pltpu.CompilerParams(vmem_limit_bytes=48*1024*1024),
    )(x,other)
    return out


def shards(record, fir_taps, source_index):
    sections = lax.axis_size("sec")
    pair = sections == 2
    sources = source_index.shape[0]
    hbm = [pltpu.with_memory_space_constraint(x, pltpu.HBM) for x in (record, fir_taps, source_index)]
    exch = share(*hbm, pair)
    filt = filter_rows(record, fir_taps)
    if pair:
        others = (exch, lax.ppermute(exch, "sec", [(0, 1), (1, 0)]))
    else:
        pilots = lax.psum(exch[:sources], "sec")
        up = [(i, i + 1) for i in range(sections - 1)]
        down = [(i + 1, i) for i in range(sections - 1)]
        high = lax.ppermute(exch[sources : sources + HALO], "sec", down)
        low = lax.ppermute(exch[sources + HALO :], "sec", up)
        others = (pilots, low, high)
    blocks = pack(filt, others, lax.axis_size("tm"), sources, pair)
    blocks = lax.all_to_all(blocks, "tm", 0, 0, tiled=True)
    swap = [(i, i ^ 1) for i in range(lax.axis_size("tm"))]
    other = lax.ppermute(blocks[:, :HALF], "tm", swap)
    return correlate(blocks, other)


def solution(mesh):
    in_specs = (P("sec", "tm"), P(), P())
    out_specs = P(("sec", "tm"), None, None)
    return jax.shard_map(shards, mesh=mesh, in_specs=in_specs, out_specs=out_specs, check_vma=False)
```

```python
import functools
import math

import jax
import jax.numpy as jnp
from jax import lax
from jax.experimental import pallas as pl
from jax.experimental.pallas import tpu as pltpu
from jax.sharding import PartitionSpec as P

f32 = jnp.float32
bf16 = jnp.bfloat16
HALF_LAG = 256
NLAG = 2 * HALF_LAG + 1
SCALE = 2.0**32
EPS = 1e-6 * SCALE * SCALE
G = 32
HALO = 32
HALF = 8
SENT = 2
FETCHES = 3


def band_halves(taps_ref, shift):
    lane = lax.broadcasted_iota(jnp.int32, (8, 256), 1)
    base = jnp.zeros((8, 256), f32)
    for m in range(taps_ref.shape[0]):
        base = jnp.where(lane == m, taps_ref[m] * SCALE, base)
    tall = jnp.concatenate([base] * 16, axis=0)
    band = pltpu.roll(tall, shift, 1, stride=1, stride_axis=0)
    high = band.astype(bf16)
    return high, (band - high.astype(f32)).astype(bf16)


def clear_edges(refs, rows):
    for ref in refs:
        deep, width = ref.shape
        ref[:64, :] = jnp.zeros((64, width), bf16)
        ref[64 + rows :, :] = jnp.zeros((deep - 64 - rows, width), bf16)


def split_rows(rec, hi_ref, lo_ref, at):
    high = rec.astype(bf16)
    hi_ref[at : at + rec.shape[0], :] = high
    lo_ref[at : at + rec.shape[0], :] = (rec - high.astype(f32)).astype(bf16)


def band_product(band, hi_ref, lo_ref, i):
    hi = hi_ref[128 * i : 128 * i + 256, :]
    lo = lo_ref[128 * i : 128 * i + 256, :]
    big = jnp.dot(jnp.concatenate(band, axis=0), hi, preferred_element_type=f32)
    small = jnp.dot(band[0], lo, preferred_element_type=f32)
    return big[:128] + (big[128:] + small)


def share_kernel(index_hbm, taps_hbm, rec_hbm, exch_ref, index_ref, taps_ref, rec_ref, sems, *, pair):
    rows, width = rec_ref.shape
    sources = index_ref.shape[0]
    taps = taps_ref.shape[0]
    step = rows // FETCHES
    fetches = [
        pltpu.make_async_copy(taps_hbm, taps_ref, sems.at[FETCHES + 1]),
        pltpu.make_async_copy(index_hbm, index_ref, sems.at[FETCHES]),
    ]
    for i in range(FETCHES):
        part = pl.ds(i * step, step)
        fetches.append(pltpu.make_async_copy(rec_hbm.at[part, :], rec_ref.at[part, :], sems.at[i]))
    for fetch in fetches:
        fetch.start()
    fetches[1].wait()
    first = lax.axis_index("sec") * rows + HALO
    at = lax.broadcasted_iota(jnp.int32, (sources, rows), 0)
    tap = jnp.zeros((sources, rows), jnp.int32)
    for s in range(sources):
        tap = jnp.where(at == s, index_ref[s] - first, tap)
    tap = lax.broadcasted_iota(jnp.int32, (sources, rows), 1) - tap
    ring = rows + 128
    lane = lax.broadcasted_iota(jnp.int32, (8, ring), 1)
    base = jnp.zeros((8, ring), f32)
    pick = jnp.zeros((sources, rows), f32)
    fetches[0].wait()
    for m in range(taps):
        value = taps_ref[m] * SCALE
        base = jnp.where(lane == m, value, base)
        pick = jnp.where(tap == m, value, pick)
    tall = jnp.concatenate([base] * (HALO // 8), axis=0)
    down = pltpu.roll(tall, ring - 64, 1, stride=1, stride_axis=0)[:, :rows]
    up = pltpu.roll(tall, rows - HALO, 1, stride=1, stride_axis=0)[:, :rows]
    edges = [jnp.where(lax.axis_index("sec") == 0, up, down)] if pair else [down, up]
    pick = jnp.concatenate([pick] + edges, axis=0)
    count = pick.shape[0]
    pick_hi = pick.astype(bf16)
    both = jnp.concatenate([pick_hi, (pick - pick_hi.astype(f32)).astype(bf16)], axis=0)
    total = jnp.zeros((count, width), f32)
    for i in range(FETCHES):
        fetches[2 + i].wait()
        part = slice(i * step, (i + 1) * step)
        rec = rec_ref[part, :]
        rec_hi = rec.astype(bf16)
        rec_lo = (rec - rec_hi.astype(f32)).astype(bf16)
        big = jnp.dot(both[:, part], rec_hi, preferred_element_type=f32)
        small = jnp.dot(pick_hi[:, part], rec_lo, preferred_element_type=f32)
        total = total + (big[:count] + (big[count:] + small))
    exch_ref[...] = total


def share(record, fir_taps, source_index, pair):
    rows, width = record.shape
    sources = source_index.shape[0]
    count = sources + HALO * (1 if pair else 2)
    return pl.pallas_call(
        functools.partial(share_kernel, pair=pair),
        out_shape=jax.ShapeDtypeStruct((count, width), f32),
        in_specs=[pl.BlockSpec(memory_space=pltpu.HBM)] * 3,
        scratch_shapes=[
            pltpu.SMEM(source_index.shape, jnp.int32),
            pltpu.SMEM(fir_taps.shape, f32),
            pltpu.VMEM((rows, width), f32),
            pltpu.SemaphoreType.DMA((FETCHES + 2,)),
        ],
        compiler_params=pltpu.CompilerParams(vmem_limit_bytes=24 * 1024 * 1024),
        cost_estimate=pl.CostEstimate(flops=6 * count * rows * width, bytes_accessed=4 * rows * width, transcendentals=0),
    )(source_index, fir_taps, record)


def filter_kernel(taps_ref, rec_ref, filt_ref, hi_ref, lo_ref):
    rows = rec_ref.shape[0]
    clear_edges((hi_ref, lo_ref), rows)
    band = band_halves(taps_ref, HALO)
    split_rows(rec_ref[...], hi_ref, lo_ref, 64)
    for i in range(rows // 128):
        filt_ref[128 * i : 128 * i + 128, :] = band_product(band, hi_ref, lo_ref, i)


def filter_rows(record, fir_taps):
    rows, width = record.shape
    return pl.pallas_call(
        filter_kernel,
        out_shape=jax.ShapeDtypeStruct((rows, width), f32),
        in_specs=[pl.BlockSpec(memory_space=pltpu.SMEM), pl.BlockSpec(memory_space=pltpu.VMEM)],
        scratch_shapes=[pltpu.VMEM((rows + 128, width), bf16), pltpu.VMEM((rows + 128, width), bf16)],
        compiler_params=pltpu.CompilerParams(vmem_limit_bytes=24 * 1024 * 1024),
        cost_estimate=pl.CostEstimate(flops=2 * 3 * rows * 256 * width, bytes_accessed=8 * rows * width, transcendentals=0),
    )(fir_taps, record)


def pack_kernel(filt_ref, *refs, count, sources, pair):
    rows = filt_ref.shape[0]
    out_ref = refs[-1]
    if pair:
        here_ref, there_ref = refs[:2]
        pilots = here_ref[:sources, :] + there_ref[:sources, :]
        edge = there_ref[sources:, :]
        second = lax.axis_index("sec") == 1
        low = jnp.where(second, edge, 0.0)
        high = jnp.where(second, 0.0, edge)
    else:
        pilots, low, high = (ref[...] for ref in refs[:3])
    for d in range(out_ref.shape[0]):
        own = pilots[HALF * (d % 2) : HALF * (d % 2) + HALF]
        lo, hi = d * count, (d + 1) * count
        part = filt_ref[lo:hi, :]
        if lo < HALO:
            n = min(hi, HALO) - lo
            add = low[lo : lo + n, :]
            part = jnp.concatenate([part[:n] + add, part[n:]], axis=0) if n < count else part + add
        if hi > rows - HALO:
            start = max(lo, rows - HALO)
            add = high[start - (rows - HALO) : hi - (rows - HALO), :]
            n = hi - start
            part = jnp.concatenate([part[: count - n], part[count - n :] + add], axis=0) if n < count else part + add
        out_ref[d] = jnp.concatenate([own, part], axis=0).astype(bf16)


def pack(filt, others, devices, sources, pair):
    rows, width = filt.shape
    count = rows // devices
    return pl.pallas_call(
        functools.partial(pack_kernel, count=count, sources=sources, pair=pair),
        out_shape=jax.ShapeDtypeStruct((devices, HALF + count, width), bf16),
        compiler_params=pltpu.CompilerParams(vmem_limit_bytes=24 * 1024 * 1024),
    )(filt, *others)


def corr_kernel(x_ref, other_ref, out_hbm, o_ref, sems, p_ref, lo_ref, v_ref, z_ref, acc_ref, *, kc, count):
    wins, _, win = x_ref.shape
    T=wins*win
    KT=T+256
    nt=T//128
    per=win//128
    esum=jnp.zeros((16,128),f32)
    usum=jnp.zeros((count,128),f32)
    zlo=jnp.zeros((16,256),bf16)
    lo_ref[:,:256]=zlo
    lo_ref[:,256+T:]=zlo[:,:128]
    v_ref[:,:128]=zlo[:,:128]
    v_ref[:,256+T:]=zlo[:,:128]
    lane8=lax.broadcasted_iota(jnp.int32,(8,128),1)
    def him(a,b):
        return jnp.concatenate([a,jnp.where(lane8<112,pltpu.roll(a,112,1),pltpu.roll(b,112,1))],axis=0).astype(bf16)
    z8=jnp.zeros((8,128),f32)
    prev=z8
    for k in range(nt):
        w,q=divmod(k,per); s=slice(q*128,q*128+128)
        block=x_ref[w,:,s].astype(f32)
        p=jnp.concatenate([block[:HALF],other_ref[w,:,s].astype(f32)],axis=0)
        u=block[HALF:]
        esum=esum+p*p; usum=usum+u*u
        p_ref[:,128*k:128*k+128]=p.astype(bf16)
        lo_ref[:,256+128*k:384+128*k]=u[:16].astype(bf16)
        v_ref[:,128+128*k:256+128*k]=him(prev,u[16:])
        prev=u[16:]
    v_ref[:,128+T:256+T]=him(prev,z8)
    lane=lax.broadcasted_iota(jnp.int32,(16,128),1)
    zp=jnp.zeros((16,128),bf16)
    for q in range(4): z_ref[q,:,:512]=jnp.zeros((16,512),bf16)
    def ptile(k):
        if k>=nt: return zp
        return p_ref[:,128*k:128*k+128]
    state=[[zp]*4,[zp]*4]
    def zbuild(k):
        t=ptile(k)
        rolls=[t]+[pltpu.roll(t,32*q,1) for q in (1,2,3)]
        S=[t]+[jnp.where(lane<32*q,state[0][q],rolls[q]) for q in (1,2,3)]
        for q in range(4): z_ref[q,:,512+128*k:640+128*k]=S[q]
        state[0]=rolls; state[1]=S
    steps=-(-KT//kc)
    def chunk(t0,first):
        X=lo_ref[:,pl.ds(t0,kc+128)]
        V=v_ref[:,pl.ds(t0,kc+128)]
        w=kc+128
        rows=[(pltpu.roll(X,w-j,1) if j else X)[:,:kc] for j in range(G+1)]
        rows+=[(pltpu.roll(V,w-j,1) if j else V)[:,:kc] for j in range(G//2)]
        rows.append(pltpu.roll(V,w-16,1)[:,:kc])
        plate=jnp.concatenate(rows,axis=0)
        rhs=jnp.concatenate([z_ref[q,:,pl.ds(t0+512-128*a,kc)] for q in range(4) for a in range(4)],axis=0)
        d=lax.dot_general(plate,rhs,(((1,),(1,)),((),())),preferred_element_type=f32)
        for a in range(2):
            if first: acc_ref[a]=d[:,128*a:128*a+128]
            else: acc_ref[a]+=d[:,128*a:128*a+128]
    for i in range(steps):
        for k in range(i*kc//128,(i+1)*kc//128): zbuild(k)
        chunk(i*kc,i==0)
    es=lax.rsqrt(jnp.sum(esum,axis=1,keepdims=True)/T+EPS)
    ue=lax.rsqrt(jnp.sum(usum,axis=1,keepdims=True)/T+EPS)/math.sqrt(T)
    esb=jnp.broadcast_to(es,(16,128))
    hi0=16*(G+1)
    mine=pl.multiple_of(lax.axis_index("tm")%2*HALF,HALF)
    theirs=pl.multiple_of(HALF-mine,HALF)
    def put(c,at,v):
        o_ref[c,pl.ds(mine,HALF),at:at+v.shape[1]]=v[:HALF]
        o_ref[c,pl.ds(theirs,HALF),at:at+v.shape[1]]=v[HALF:]
    def lags(h,c):
        if c<16: return acc_ref[h,pl.ds(c,32,stride=16),:]
        return jnp.concatenate([acc_ref[h,pl.ds(hi0+c-16,16,stride=16),:],acc_ref[h,pl.ds(hi0+c-8,16,stride=16),:]],axis=0)
    last=jnp.concatenate([acc_ref[1,512:528,:],acc_ref[1,hi0+264:hi0+272,:]],axis=0)
    last=jnp.concatenate([last*ue,jnp.zeros((104,128),f32)],axis=0).T[112:128]*es
    for c in range(count):
        v=pltpu.roll(last,128-c,1) if c else last
        put(c,512,v[:,0:1])
    copies=[]
    wide=lax.broadcasted_iota(jnp.int32,(32,128),1)<64
    for c in range(0,count,2):
        parts=[]
        for h in range(2):
            even,odd=lags(h,c),lags(h,c+1)
            crossed=pltpu.roll(jnp.where(wide,odd,even),64,1)
            parts.append(jnp.where(wide,even,crossed))
            parts.append(jnp.where(wide,crossed,odd))
        turned=jnp.concatenate(parts,axis=0).T
        for m in range(2):
            scl=esb*jnp.broadcast_to(ue[c+m:c+m+1],(16,128))
            for a in range(4):
                put(c+m,128*a,turned[64*m+16*a:64*m+16*a+16,:]*scl)
        if (c+2)%SENT==0:
            group=pl.ds(c+2-SENT,SENT)
            copies.append(pltpu.make_async_copy(o_ref.at[group],out_hbm.at[group],sems.at[c//SENT]))
            copies[-1].start()
    for copy in copies:
        copy.wait()


def correlate(x,other):
    wins,rows,win=x.shape
    count=rows-HALF
    T=wins*win
    kc=T+256
    out=pl.pallas_call(functools.partial(corr_kernel,kc=kc,count=count),
        out_shape=jax.ShapeDtypeStruct((count,16,NLAG),f32),
        out_specs=pl.BlockSpec(memory_space=pltpu.HBM),
        scratch_shapes=[pltpu.VMEM((count,16,NLAG),f32),pltpu.SemaphoreType.DMA((count//SENT,)),pltpu.VMEM((16,T),bf16),pltpu.VMEM((16,T+384),bf16),pltpu.VMEM((16,T+384),bf16),pltpu.VMEM((4,16,T+768),bf16),pltpu.VMEM((2,16*(3*G//2+2),128),f32)],
        compiler_params=pltpu.CompilerParams(vmem_limit_bytes=48*1024*1024),
    )(x,other)
    return out


def shards(record, fir_taps, source_index):
    sections = lax.axis_size("sec")
    pair = sections == 2
    sources = source_index.shape[0]
    hbm = [pltpu.with_memory_space_constraint(x, pltpu.HBM) for x in (record, fir_taps, source_index)]
    exch = share(*hbm, pair)
    filt = filter_rows(record, fir_taps)
    if pair:
        others = (exch, lax.ppermute(exch, "sec", [(0, 1), (1, 0)]))
    else:
        pilots = lax.psum(exch[:sources], "sec")
        up = [(i, i + 1) for i in range(sections - 1)]
        down = [(i + 1, i) for i in range(sections - 1)]
        high = lax.ppermute(exch[sources : sources + HALO], "sec", down)
        low = lax.ppermute(exch[sources + HALO :], "sec", up)
        others = (pilots, low, high)
    blocks = pack(filt, others, lax.axis_size("tm"), sources, pair)
    blocks = lax.all_to_all(blocks, "tm", 0, 0, tiled=True)
    swap = [(i, i ^ 1) for i in range(lax.axis_size("tm"))]
    other = lax.ppermute(blocks[:, :HALF], "tm", swap)
    return correlate(blocks, other)


def solution(mesh):
    in_specs = (P("sec", "tm"), P(), P())
    out_specs = P(("sec", "tm"), None, None)
    return jax.shard_map(shards, mesh=mesh, in_specs=in_specs, out_specs=out_specs, check_vma=False)
```

```python
import functools
import math

import jax
import jax.numpy as jnp
from jax import lax
from jax.experimental import pallas as pl
from jax.experimental.pallas import tpu as pltpu
from jax.sharding import PartitionSpec as P

f32 = jnp.float32
bf16 = jnp.bfloat16
HALF_LAG = 256
NLAG = 2 * HALF_LAG + 1
SCALE = 2.0**32
EPS = 1e-6 * SCALE * SCALE
G = 32
HALO = 32
HALF = 8
SENT = 2
AHEAD = 1
FETCHES = 3


def band_halves(taps_ref, shift):
    lane = lax.broadcasted_iota(jnp.int32, (8, 256), 1)
    base = jnp.zeros((8, 256), f32)
    for m in range(taps_ref.shape[0]):
        base = jnp.where(lane == m, taps_ref[m] * SCALE, base)
    tall = jnp.concatenate([base] * 16, axis=0)
    band = pltpu.roll(tall, shift, 1, stride=1, stride_axis=0)
    high = band.astype(bf16)
    return high, (band - high.astype(f32)).astype(bf16)


def clear_edges(refs, rows):
    for ref in refs:
        deep, width = ref.shape
        ref[:64, :] = jnp.zeros((64, width), bf16)
        ref[64 + rows :, :] = jnp.zeros((deep - 64 - rows, width), bf16)


def split_rows(rec, hi_ref, lo_ref, at):
    high = rec.astype(bf16)
    hi_ref[at : at + rec.shape[0], :] = high
    lo_ref[at : at + rec.shape[0], :] = (rec - high.astype(f32)).astype(bf16)


def band_product(band, hi_ref, lo_ref, i):
    hi = hi_ref[128 * i : 128 * i + 256, :]
    lo = lo_ref[128 * i : 128 * i + 256, :]
    big = jnp.dot(jnp.concatenate(band, axis=0), hi, preferred_element_type=f32)
    small = jnp.dot(band[0], lo, preferred_element_type=f32)
    return big[:128] + (big[128:] + small)


def share_kernel(index_hbm, taps_hbm, rec_hbm, exch_ref, index_ref, taps_ref, rec_ref, sems, *, pair):
    rows, width = rec_ref.shape
    sources = index_ref.shape[0]
    taps = taps_ref.shape[0]
    step = rows // FETCHES
    fetches = [
        pltpu.make_async_copy(taps_hbm, taps_ref, sems.at[FETCHES + 1]),
        pltpu.make_async_copy(index_hbm, index_ref, sems.at[FETCHES]),
    ]
    for i in range(FETCHES):
        part = pl.ds(i * step, step)
        fetches.append(pltpu.make_async_copy(rec_hbm.at[part, :], rec_ref.at[part, :], sems.at[i]))
    for fetch in fetches:
        fetch.start()
    fetches[1].wait()
    first = lax.axis_index("sec") * rows + HALO
    at = lax.broadcasted_iota(jnp.int32, (sources, rows), 0)
    tap = jnp.zeros((sources, rows), jnp.int32)
    for s in range(sources):
        tap = jnp.where(at == s, index_ref[s] - first, tap)
    tap = lax.broadcasted_iota(jnp.int32, (sources, rows), 1) - tap
    ring = rows + 128
    lane = lax.broadcasted_iota(jnp.int32, (8, ring), 1)
    base = jnp.zeros((8, ring), f32)
    pick = jnp.zeros((sources, rows), f32)
    fetches[0].wait()
    for m in range(taps):
        value = taps_ref[m] * SCALE
        base = jnp.where(lane == m, value, base)
        pick = jnp.where(tap == m, value, pick)
    tall = jnp.concatenate([base] * (HALO // 8), axis=0)
    down = pltpu.roll(tall, ring - 64, 1, stride=1, stride_axis=0)[:, :rows]
    up = pltpu.roll(tall, rows - HALO, 1, stride=1, stride_axis=0)[:, :rows]
    edges = [jnp.where(lax.axis_index("sec") == 0, up, down)] if pair else [down, up]
    pick = jnp.concatenate([pick] + edges, axis=0)
    count = pick.shape[0]
    pick_hi = pick.astype(bf16)
    both = jnp.concatenate([pick_hi, (pick - pick_hi.astype(f32)).astype(bf16)], axis=0)
    total = jnp.zeros((count, width), f32)
    for i in range(FETCHES):
        fetches[2 + i].wait()
        part = slice(i * step, (i + 1) * step)
        rec = rec_ref[part, :]
        rec_hi = rec.astype(bf16)
        rec_lo = (rec - rec_hi.astype(f32)).astype(bf16)
        big = jnp.dot(both[:, part], rec_hi, preferred_element_type=f32)
        small = jnp.dot(pick_hi[:, part], rec_lo, preferred_element_type=f32)
        total = total + (big[:count] + (big[count:] + small))
    exch_ref[...] = total


def share(record, fir_taps, source_index, pair):
    rows, width = record.shape
    sources = source_index.shape[0]
    count = sources + HALO * (1 if pair else 2)
    return pl.pallas_call(
        functools.partial(share_kernel, pair=pair),
        out_shape=jax.ShapeDtypeStruct((count, width), f32),
        in_specs=[pl.BlockSpec(memory_space=pltpu.HBM)] * 3,
        scratch_shapes=[
            pltpu.SMEM(source_index.shape, jnp.int32),
            pltpu.SMEM(fir_taps.shape, f32),
            pltpu.VMEM((rows, width), f32),
            pltpu.SemaphoreType.DMA((FETCHES + 2,)),
        ],
        compiler_params=pltpu.CompilerParams(vmem_limit_bytes=24 * 1024 * 1024),
        cost_estimate=pl.CostEstimate(flops=6 * count * rows * width, bytes_accessed=4 * rows * width, transcendentals=0),
    )(source_index, fir_taps, record)


def filter_kernel(taps_ref, rec_ref, filt_ref, hi_ref, lo_ref):
    rows = rec_ref.shape[0]
    clear_edges((hi_ref, lo_ref), rows)
    band = band_halves(taps_ref, HALO)
    split_rows(rec_ref[...], hi_ref, lo_ref, 64)
    for i in range(rows // 128):
        filt_ref[128 * i : 128 * i + 128, :] = band_product(band, hi_ref, lo_ref, i)


def filter_rows(record, fir_taps):
    rows, width = record.shape
    return pl.pallas_call(
        filter_kernel,
        out_shape=jax.ShapeDtypeStruct((rows, width), f32),
        in_specs=[pl.BlockSpec(memory_space=pltpu.SMEM), pl.BlockSpec(memory_space=pltpu.VMEM)],
        scratch_shapes=[pltpu.VMEM((rows + 128, width), bf16), pltpu.VMEM((rows + 128, width), bf16)],
        compiler_params=pltpu.CompilerParams(vmem_limit_bytes=24 * 1024 * 1024),
        cost_estimate=pl.CostEstimate(flops=2 * 3 * rows * 256 * width, bytes_accessed=8 * rows * width, transcendentals=0),
    )(fir_taps, record)


def pack_kernel(filt_ref, *refs, count, sources, pair):
    rows = filt_ref.shape[0]
    out_ref = refs[-1]
    if pair:
        here_ref, there_ref = refs[:2]
        pilots = here_ref[:sources, :] + there_ref[:sources, :]
        edge = there_ref[sources:, :]
        second = lax.axis_index("sec") == 1
        low = jnp.where(second, edge, 0.0)
        high = jnp.where(second, 0.0, edge)
    else:
        pilots, low, high = (ref[...] for ref in refs[:3])
    for d in range(out_ref.shape[0]):
        own = pilots[HALF * (d % 2) : HALF * (d % 2) + HALF]
        lo, hi = d * count, (d + 1) * count
        part = filt_ref[lo:hi, :]
        if lo < HALO:
            n = min(hi, HALO) - lo
            add = low[lo : lo + n, :]
            part = jnp.concatenate([part[:n] + add, part[n:]], axis=0) if n < count else part + add
        if hi > rows - HALO:
            start = max(lo, rows - HALO)
            add = high[start - (rows - HALO) : hi - (rows - HALO), :]
            n = hi - start
            part = jnp.concatenate([part[: count - n], part[count - n :] + add], axis=0) if n < count else part + add
        out_ref[d] = jnp.concatenate([own, part], axis=0).astype(bf16)


def pack(filt, others, devices, sources, pair):
    rows, width = filt.shape
    count = rows // devices
    return pl.pallas_call(
        functools.partial(pack_kernel, count=count, sources=sources, pair=pair),
        out_shape=jax.ShapeDtypeStruct((devices, HALF + count, width), bf16),
        compiler_params=pltpu.CompilerParams(vmem_limit_bytes=24 * 1024 * 1024),
    )(filt, *others)


def ready_kernel(x_ref, plate_ref, lo_ref, sum_ref, v_ref, *, count):
    wins, _, win = x_ref.shape
    T = wins * win
    KT = T + 256
    per = win // 128
    usum = jnp.zeros((count, 128), f32)
    blank = jnp.zeros((16, 256), bf16)
    lo_ref[:, :256] = blank
    lo_ref[:, 256 + T :] = blank[:, :128]
    v_ref[:, :128] = blank[:, :128]
    v_ref[:, 256 + T :] = blank[:, :128]
    lane8 = lax.broadcasted_iota(jnp.int32, (8, 128), 1)

    def paired(a, b):
        later = jnp.where(lane8 < 112, pltpu.roll(a, 112, 1), pltpu.roll(b, 112, 1))
        return jnp.concatenate([a, later], axis=0).astype(bf16)

    none = jnp.zeros((8, 128), f32)
    prev = none
    for k in range(T // 128):
        w, q = divmod(k, per)
        u = x_ref[w, :, q * 128 : q * 128 + 128].astype(f32)[HALF:]
        usum = usum + u * u
        lo_ref[:, 256 + 128 * k : 384 + 128 * k] = u[:16].astype(bf16)
        v_ref[:, 128 + 128 * k : 256 + 128 * k] = paired(prev, u[16:])
        prev = u[16:]
    v_ref[:, 128 + T : 256 + T] = paired(prev, none)
    sum_ref[...] = usum
    w = KT + 128
    V = v_ref[...]
    for j in range(G // 2 + 1):
        plate_ref[16 * j : 16 * j + 16, :] = (pltpu.roll(V, w - j, 1) if j else V)[:, :KT]
    X = lo_ref[...]
    for n in range(AHEAD):
        at = 16 * (G // 2 + 1 + n)
        plate_ref[at : at + 16, :] = pltpu.roll(X, w - (G - n), 1)[:, :KT]


def make_ready(x):
    wins, rows, win = x.shape
    T = wins * win
    return pl.pallas_call(
        functools.partial(ready_kernel, count=rows - HALF),
        out_shape=(
            jax.ShapeDtypeStruct((16 * (G // 2 + 1 + AHEAD), T + 256), bf16),
            jax.ShapeDtypeStruct((16, T + 384), bf16),
            jax.ShapeDtypeStruct((rows - HALF, 128), f32),
        ),
        scratch_shapes=[pltpu.VMEM((16, T + 384), bf16)],
        compiler_params=pltpu.CompilerParams(vmem_limit_bytes=16 * 1024 * 1024),
        cost_estimate=pl.CostEstimate(flops=20 * 16 * T, bytes_accessed=40 * 16 * T, transcendentals=0),
    )(x)


def corr_kernel(x_ref, other_ref, ready_ref, lo_ref, sum_ref, out_hbm, o_ref, sems, p_ref, z_ref, acc_ref, *, kc, count):
    wins, _, win = x_ref.shape
    T=wins*win
    KT=T+256
    nt=T//128
    per=win//128
    esum=jnp.zeros((16,128),f32)
    for k in range(nt):
        w,q=divmod(k,per); s=slice(q*128,q*128+128)
        near=x_ref[w,:,s].astype(f32)[:HALF]
        p=jnp.concatenate([near,other_ref[w,:,s].astype(f32)],axis=0)
        esum=esum+p*p
        p_ref[:,128*k:128*k+128]=p.astype(bf16)
    usum=sum_ref[...]
    lane=lax.broadcasted_iota(jnp.int32,(16,128),1)
    zp=jnp.zeros((16,128),bf16)
    for q in range(4): z_ref[q,:,:512]=jnp.zeros((16,512),bf16)
    def ptile(k):
        if k>=nt: return zp
        return p_ref[:,128*k:128*k+128]
    state=[[zp]*4,[zp]*4]
    def zbuild(k):
        t=ptile(k)
        rolls=[t]+[pltpu.roll(t,32*q,1) for q in (1,2,3)]
        S=[t]+[jnp.where(lane<32*q,state[0][q],rolls[q]) for q in (1,2,3)]
        for q in range(4): z_ref[q,:,512+128*k:640+128*k]=S[q]
        state[0]=rolls; state[1]=S
    steps=-(-KT//kc)
    def chunk(t0,first):
        X=lo_ref[...]
        w=kc+128
        tail=16*(G//2+1)
        rows=[(pltpu.roll(X,w-j,1) if j else X)[:,:kc] for j in range(G+1-AHEAD)]
        rows+=[ready_ref[tail+16*n:tail+16*n+16,:] for n in range(AHEAD-1,-1,-1)]
        rows.append(ready_ref[:tail,:])
        plate=jnp.concatenate(rows,axis=0)
        rhs=jnp.concatenate([z_ref[q,:,pl.ds(t0+512-128*a,kc)] for q in range(4) for a in range(4)],axis=0)
        d=lax.dot_general(plate,rhs,(((1,),(1,)),((),())),preferred_element_type=f32)
        for a in range(2):
            if first: acc_ref[a]=d[:,128*a:128*a+128]
            else: acc_ref[a]+=d[:,128*a:128*a+128]
    for i in range(steps):
        for k in range(i*kc//128,(i+1)*kc//128): zbuild(k)
        chunk(i*kc,i==0)
    es=lax.rsqrt(jnp.sum(esum,axis=1,keepdims=True)/T+EPS)
    ue=lax.rsqrt(jnp.sum(usum,axis=1,keepdims=True)/T+EPS)/math.sqrt(T)
    esb=jnp.broadcast_to(es,(16,128))
    hi0=16*(G+1)
    mine=pl.multiple_of(lax.axis_index("tm")%2*HALF,HALF)
    theirs=pl.multiple_of(HALF-mine,HALF)
    def put(c,at,v):
        o_ref[c,pl.ds(mine,HALF),at:at+v.shape[1]]=v[:HALF]
        o_ref[c,pl.ds(theirs,HALF),at:at+v.shape[1]]=v[HALF:]
    def lags(h,c):
        if c<16: return acc_ref[h,pl.ds(c,32,stride=16),:]
        return jnp.concatenate([acc_ref[h,pl.ds(hi0+c-16,16,stride=16),:],acc_ref[h,pl.ds(hi0+c-8,16,stride=16),:]],axis=0)
    last=jnp.concatenate([acc_ref[1,512:528,:],acc_ref[1,hi0+264:hi0+272,:]],axis=0)
    last=jnp.concatenate([last*ue,jnp.zeros((104,128),f32)],axis=0).T[112:128]*es
    for c in range(count):
        v=pltpu.roll(last,128-c,1) if c else last
        put(c,512,v[:,0:1])
    copies=[]
    wide=lax.broadcasted_iota(jnp.int32,(32,128),1)<64
    for c in range(0,count,2):
        parts=[]
        for h in range(2):
            even,odd=lags(h,c),lags(h,c+1)
            crossed=pltpu.roll(jnp.where(wide,odd,even),64,1)
            parts.append(jnp.where(wide,even,crossed))
            parts.append(jnp.where(wide,crossed,odd))
        turned=jnp.concatenate(parts,axis=0).T
        for m in range(2):
            scl=esb*jnp.broadcast_to(ue[c+m:c+m+1],(16,128))
            for a in range(4):
                put(c+m,128*a,turned[64*m+16*a:64*m+16*a+16,:]*scl)
        if (c+2)%SENT==0:
            group=pl.ds(c+2-SENT,SENT)
            copies.append(pltpu.make_async_copy(o_ref.at[group],out_hbm.at[group],sems.at[c//SENT]))
            copies[-1].start()
    for copy in copies:
        copy.wait()


def correlate(x,other,ready):
    wins,rows,win=x.shape
    count=rows-HALF
    T=wins*win
    kc=T+256
    out=pl.pallas_call(functools.partial(corr_kernel,kc=kc,count=count),
        out_shape=jax.ShapeDtypeStruct((count,16,NLAG),f32),
        out_specs=pl.BlockSpec(memory_space=pltpu.HBM),
        scratch_shapes=[pltpu.VMEM((count,16,NLAG),f32),pltpu.SemaphoreType.DMA((count//SENT,)),pltpu.VMEM((16,T),bf16),pltpu.VMEM((4,16,T+768),bf16),pltpu.VMEM((2,16*(3*G//2+2),128),f32)],
        compiler_params=pltpu.CompilerParams(vmem_limit_bytes=36*1024*1024),
    )(x,other,*ready)
    return out


def shards(record, fir_taps, source_index):
    sections = lax.axis_size("sec")
    pair = sections == 2
    sources = source_index.shape[0]
    hbm = [pltpu.with_memory_space_constraint(x, pltpu.HBM) for x in (record, fir_taps, source_index)]
    exch = share(*hbm, pair)
    filt = filter_rows(record, fir_taps)
    if pair:
        others = (exch, lax.ppermute(exch, "sec", [(0, 1), (1, 0)]))
    else:
        pilots = lax.psum(exch[:sources], "sec")
        up = [(i, i + 1) for i in range(sections - 1)]
        down = [(i + 1, i) for i in range(sections - 1)]
        high = lax.ppermute(exch[sources : sources + HALO], "sec", down)
        low = lax.ppermute(exch[sources + HALO :], "sec", up)
        others = (pilots, low, high)
    blocks = pack(filt, others, lax.axis_size("tm"), sources, pair)
    blocks = lax.all_to_all(blocks, "tm", 0, 0, tiled=True)
    swap = [(i, i ^ 1) for i in range(lax.axis_size("tm"))]
    other = lax.ppermute(blocks[:, :HALF], "tm", swap)
    return correlate(blocks, other, make_ready(blocks))


def solution(mesh):
    in_specs = (P("sec", "tm"), P(), P())
    out_specs = P(("sec", "tm"), None, None)
    return jax.shard_map(shards, mesh=mesh, in_specs=in_specs, out_specs=out_specs, check_vma=False)
```

```python
import functools
import math

import jax
import jax.numpy as jnp
from jax import lax
from jax.experimental import pallas as pl
from jax.experimental.pallas import tpu as pltpu
from jax.sharding import PartitionSpec as P

f32 = jnp.float32
bf16 = jnp.bfloat16
HALF_LAG = 256
NLAG = 2 * HALF_LAG + 1
SCALE = 2.0**32
EPS = 1e-6 * SCALE * SCALE
G = 32
HALO = 32
HALF = 8
SENT = 2
FETCHES = 3


def band_halves(taps_ref, shift):
    lane = lax.broadcasted_iota(jnp.int32, (8, 256), 1)
    base = jnp.zeros((8, 256), f32)
    for m in range(taps_ref.shape[0]):
        base = jnp.where(lane == m, taps_ref[m] * SCALE, base)
    tall = jnp.concatenate([base] * 16, axis=0)
    band = pltpu.roll(tall, shift, 1, stride=1, stride_axis=0)
    high = band.astype(bf16)
    return high, (band - high.astype(f32)).astype(bf16)


def clear_edges(refs, rows):
    for ref in refs:
        deep, width = ref.shape
        ref[:64, :] = jnp.zeros((64, width), bf16)
        ref[64 + rows :, :] = jnp.zeros((deep - 64 - rows, width), bf16)


def split_rows(rec, hi_ref, lo_ref, at):
    high = rec.astype(bf16)
    hi_ref[at : at + rec.shape[0], :] = high
    lo_ref[at : at + rec.shape[0], :] = (rec - high.astype(f32)).astype(bf16)


def band_product(band, hi_ref, lo_ref, i):
    hi = hi_ref[128 * i : 128 * i + 256, :]
    lo = lo_ref[128 * i : 128 * i + 256, :]
    big = jnp.dot(jnp.concatenate(band, axis=0), hi, preferred_element_type=f32)
    small = jnp.dot(band[0], lo, preferred_element_type=f32)
    return big[:128] + (big[128:] + small)


def share_kernel(index_hbm, taps_hbm, rec_hbm, exch_ref, index_ref, taps_ref, rec_ref, sems, *, pair):
    rows, width = rec_ref.shape
    sources = index_ref.shape[0]
    taps = taps_ref.shape[0]
    step = rows // FETCHES
    fetches = [
        pltpu.make_async_copy(taps_hbm, taps_ref, sems.at[FETCHES + 1]),
        pltpu.make_async_copy(index_hbm, index_ref, sems.at[FETCHES]),
    ]
    for i in range(FETCHES):
        part = pl.ds(i * step, step)
        fetches.append(pltpu.make_async_copy(rec_hbm.at[part, :], rec_ref.at[part, :], sems.at[i]))
    for fetch in fetches:
        fetch.start()
    fetches[1].wait()
    first = lax.axis_index("sec") * rows + HALO
    at = lax.broadcasted_iota(jnp.int32, (sources, rows), 0)
    tap = jnp.zeros((sources, rows), jnp.int32)
    for s in range(sources):
        tap = jnp.where(at == s, index_ref[s] - first, tap)
    tap = lax.broadcasted_iota(jnp.int32, (sources, rows), 1) - tap
    ring = rows + 128
    lane = lax.broadcasted_iota(jnp.int32, (8, ring), 1)
    base = jnp.zeros((8, ring), f32)
    pick = jnp.zeros((sources, rows), f32)
    fetches[0].wait()
    for m in range(taps):
        value = taps_ref[m] * SCALE
        base = jnp.where(lane == m, value, base)
        pick = jnp.where(tap == m, value, pick)
    tall = jnp.concatenate([base] * (HALO // 8), axis=0)
    down = pltpu.roll(tall, ring - 64, 1, stride=1, stride_axis=0)[:, :rows]
    up = pltpu.roll(tall, rows - HALO, 1, stride=1, stride_axis=0)[:, :rows]
    edges = [jnp.where(lax.axis_index("sec") == 0, up, down)] if pair else [down, up]
    pick = jnp.concatenate([pick] + edges, axis=0)
    count = pick.shape[0]
    pick_hi = pick.astype(bf16)
    both = jnp.concatenate([pick_hi, (pick - pick_hi.astype(f32)).astype(bf16)], axis=0)
    total = jnp.zeros((count, width), f32)
    for i in range(FETCHES):
        fetches[2 + i].wait()
        part = slice(i * step, (i + 1) * step)
        rec = rec_ref[part, :]
        rec_hi = rec.astype(bf16)
        rec_lo = (rec - rec_hi.astype(f32)).astype(bf16)
        big = jnp.dot(both[:, part], rec_hi, preferred_element_type=f32)
        small = jnp.dot(pick_hi[:, part], rec_lo, preferred_element_type=f32)
        total = total + (big[:count] + (big[count:] + small))
    exch_ref[...] = total


def share(record, fir_taps, source_index, pair):
    rows, width = record.shape
    sources = source_index.shape[0]
    count = sources + HALO * (1 if pair else 2)
    return pl.pallas_call(
        functools.partial(share_kernel, pair=pair),
        out_shape=jax.ShapeDtypeStruct((count, width), f32),
        in_specs=[pl.BlockSpec(memory_space=pltpu.HBM)] * 3,
        scratch_shapes=[
            pltpu.SMEM(source_index.shape, jnp.int32),
            pltpu.SMEM(fir_taps.shape, f32),
            pltpu.VMEM((rows, width), f32),
            pltpu.SemaphoreType.DMA((FETCHES + 2,)),
        ],
        compiler_params=pltpu.CompilerParams(vmem_limit_bytes=24 * 1024 * 1024),
        cost_estimate=pl.CostEstimate(flops=6 * count * rows * width, bytes_accessed=4 * rows * width, transcendentals=0),
    )(source_index, fir_taps, record)


def filter_kernel(taps_ref, rec_ref, filt_ref, hi_ref, lo_ref):
    rows = rec_ref.shape[0]
    clear_edges((hi_ref, lo_ref), rows)
    band = band_halves(taps_ref, HALO)
    split_rows(rec_ref[...], hi_ref, lo_ref, 64)
    for i in range(rows // 128):
        filt_ref[128 * i : 128 * i + 128, :] = band_product(band, hi_ref, lo_ref, i)


def filter_rows(record, fir_taps):
    rows, width = record.shape
    return pl.pallas_call(
        filter_kernel,
        out_shape=jax.ShapeDtypeStruct((rows, width), f32),
        in_specs=[pl.BlockSpec(memory_space=pltpu.SMEM), pl.BlockSpec(memory_space=pltpu.VMEM)],
        scratch_shapes=[pltpu.VMEM((rows + 128, width), bf16), pltpu.VMEM((rows + 128, width), bf16)],
        compiler_params=pltpu.CompilerParams(vmem_limit_bytes=24 * 1024 * 1024),
        cost_estimate=pl.CostEstimate(flops=2 * 3 * rows * 256 * width, bytes_accessed=8 * rows * width, transcendentals=0),
    )(fir_taps, record)


def pack_kernel(filt_ref, *refs, count, sources, pair):
    rows = filt_ref.shape[0]
    out_ref = refs[-1]
    if pair:
        here_ref, there_ref = refs[:2]
        pilots = here_ref[:sources, :] + there_ref[:sources, :]
        edge = there_ref[sources:, :]
        second = lax.axis_index("sec") == 1
        low = jnp.where(second, edge, 0.0)
        high = jnp.where(second, 0.0, edge)
    else:
        pilots, low, high = (ref[...] for ref in refs[:3])
    for d in range(out_ref.shape[0]):
        own = pilots[HALF * (d % 2) : HALF * (d % 2) + HALF]
        lo, hi = d * count, (d + 1) * count
        part = filt_ref[lo:hi, :]
        if lo < HALO:
            n = min(hi, HALO) - lo
            add = low[lo : lo + n, :]
            part = jnp.concatenate([part[:n] + add, part[n:]], axis=0) if n < count else part + add
        if hi > rows - HALO:
            start = max(lo, rows - HALO)
            add = high[start - (rows - HALO) : hi - (rows - HALO), :]
            n = hi - start
            part = jnp.concatenate([part[: count - n], part[count - n :] + add], axis=0) if n < count else part + add
        out_ref[d] = jnp.concatenate([own, part], axis=0).astype(bf16)


def pack(filt, others, devices, sources, pair):
    rows, width = filt.shape
    count = rows // devices
    return pl.pallas_call(
        functools.partial(pack_kernel, count=count, sources=sources, pair=pair),
        out_shape=jax.ShapeDtypeStruct((devices, HALF + count, width), bf16),
        compiler_params=pltpu.CompilerParams(vmem_limit_bytes=24 * 1024 * 1024),
    )(filt, *others)


def ready_kernel(x_ref, plate_ref, lo_ref, sum_ref, v_ref, *, count):
    wins, _, win = x_ref.shape
    T = wins * win
    KT = T + 256
    per = win // 128
    usum = jnp.zeros((count, 128), f32)
    blank = jnp.zeros((16, 256), bf16)
    lo_ref[:, :256] = blank
    lo_ref[:, 256 + T :] = blank[:, :128]
    v_ref[:, :128] = blank[:, :128]
    v_ref[:, 256 + T :] = blank[:, :128]
    lane8 = lax.broadcasted_iota(jnp.int32, (8, 128), 1)

    def paired(a, b):
        later = jnp.where(lane8 < 112, pltpu.roll(a, 112, 1), pltpu.roll(b, 112, 1))
        return jnp.concatenate([a, later], axis=0).astype(bf16)

    none = jnp.zeros((8, 128), f32)
    prev = none
    for k in range(T // 128):
        w, q = divmod(k, per)
        u = x_ref[w, :, q * 128 : q * 128 + 128].astype(f32)[HALF:]
        usum = usum + u * u
        lo_ref[:, 256 + 128 * k : 384 + 128 * k] = u[:16].astype(bf16)
        v_ref[:, 128 + 128 * k : 256 + 128 * k] = paired(prev, u[16:])
        prev = u[16:]
    v_ref[:, 128 + T : 256 + T] = paired(prev, none)
    sum_ref[...] = usum
    w = KT + 128
    V = v_ref[...]
    for j in range(G // 2 + 1):
        plate_ref[16 * j : 16 * j + 16, :] = (pltpu.roll(V, w - j, 1) if j else V)[:, :KT]


def make_ready(x):
    wins, rows, win = x.shape
    T = wins * win
    return pl.pallas_call(
        functools.partial(ready_kernel, count=rows - HALF),
        out_shape=(
            jax.ShapeDtypeStruct((16 * (G // 2 + 1), T + 256), bf16),
            jax.ShapeDtypeStruct((16, T + 384), bf16),
            jax.ShapeDtypeStruct((rows - HALF, 128), f32),
        ),
        scratch_shapes=[pltpu.VMEM((16, T + 384), bf16)],
        compiler_params=pltpu.CompilerParams(vmem_limit_bytes=16 * 1024 * 1024),
        cost_estimate=pl.CostEstimate(flops=20 * 16 * T, bytes_accessed=40 * 16 * T, transcendentals=0),
    )(x)


def corr_kernel(x_ref, other_ref, ready_ref, lo_ref, sum_ref, out_hbm, o_ref, sems, p_ref, z_ref, acc_ref, *, kc, count):
    wins, _, win = x_ref.shape
    T=wins*win
    KT=T+256
    nt=T//128
    per=win//128
    esum=jnp.zeros((16,128),f32)
    for k in range(nt):
        w,q=divmod(k,per); s=slice(q*128,q*128+128)
        near=x_ref[w,:,s].astype(f32)[:HALF]
        p=jnp.concatenate([near,other_ref[w,:,s].astype(f32)],axis=0)
        esum=esum+p*p
        p_ref[:,128*k:128*k+128]=p.astype(bf16)
    usum=sum_ref[...]
    lane=lax.broadcasted_iota(jnp.int32,(16,128),1)
    zp=jnp.zeros((16,128),bf16)
    for q in range(4): z_ref[q,:,:512]=jnp.zeros((16,512),bf16)
    def ptile(k):
        if k>=nt: return zp
        return p_ref[:,128*k:128*k+128]
    state=[[zp]*4,[zp]*4]
    def zbuild(k):
        t=ptile(k)
        rolls=[t]+[pltpu.roll(t,32*q,1) for q in (1,2,3)]
        S=[t]+[jnp.where(lane<32*q,state[0][q],rolls[q]) for q in (1,2,3)]
        for q in range(4): z_ref[q,:,512+128*k:640+128*k]=S[q]
        state[0]=rolls; state[1]=S
    steps=-(-KT//kc)
    def chunk(t0,first):
        X=lo_ref[...]
        w=kc+128
        rows=[(pltpu.roll(X,w-j,1) if j else X)[:,:kc] for j in range(G+1)]
        rows.append(ready_ref[...])
        plate=jnp.concatenate(rows,axis=0)
        rhs=jnp.concatenate([z_ref[q,:,pl.ds(t0+512-128*a,kc)] for q in range(4) for a in range(4)],axis=0)
        d=lax.dot_general(plate,rhs,(((1,),(1,)),((),())),preferred_element_type=f32)
        for a in range(2):
            if first: acc_ref[a]=d[:,128*a:128*a+128]
            else: acc_ref[a]+=d[:,128*a:128*a+128]
    for i in range(steps):
        for k in range(i*kc//128,(i+1)*kc//128): zbuild(k)
        chunk(i*kc,i==0)
    es=lax.rsqrt(jnp.sum(esum,axis=1,keepdims=True)/T+EPS)
    ue=lax.rsqrt(jnp.sum(usum,axis=1,keepdims=True)/T+EPS)/math.sqrt(T)
    esb=jnp.broadcast_to(es,(16,128))
    hi0=16*(G+1)
    mine=pl.multiple_of(lax.axis_index("tm")%2*HALF,HALF)
    theirs=pl.multiple_of(HALF-mine,HALF)
    def put(c,at,v):
        o_ref[c,pl.ds(mine,HALF),at:at+v.shape[1]]=v[:HALF]
        o_ref[c,pl.ds(theirs,HALF),at:at+v.shape[1]]=v[HALF:]
    def lags(h,c):
        if c<16: return acc_ref[h,pl.ds(c,32,stride=16),:]
        return jnp.concatenate([acc_ref[h,pl.ds(hi0+c-16,16,stride=16),:],acc_ref[h,pl.ds(hi0+c-8,16,stride=16),:]],axis=0)
    last=jnp.concatenate([acc_ref[1,512:528,:],acc_ref[1,hi0+264:hi0+272,:]],axis=0)
    last=jnp.concatenate([last*ue,jnp.zeros((104,128),f32)],axis=0).T[112:128]*es
    for c in range(count):
        v=pltpu.roll(last,128-c,1) if c else last
        put(c,512,v[:,0:1])
    copies=[]
    wide=lax.broadcasted_iota(jnp.int32,(32,128),1)<64
    for c in range(0,count,2):
        parts=[]
        for h in range(2):
            even,odd=lags(h,c),lags(h,c+1)
            crossed=pltpu.roll(jnp.where(wide,odd,even),64,1)
            parts.append(jnp.where(wide,even,crossed))
            parts.append(jnp.where(wide,crossed,odd))
        turned=jnp.concatenate(parts,axis=0).T
        for m in range(2):
            scl=esb*jnp.broadcast_to(ue[c+m:c+m+1],(16,128))
            for a in range(4):
                put(c+m,128*a,turned[64*m+16*a:64*m+16*a+16,:]*scl)
        if (c+2)%SENT==0:
            group=pl.ds(c+2-SENT,SENT)
            copies.append(pltpu.make_async_copy(o_ref.at[group],out_hbm.at[group],sems.at[c//SENT]))
            copies[-1].start()
    for copy in copies:
        copy.wait()


def correlate(x,other,ready):
    wins,rows,win=x.shape
    count=rows-HALF
    T=wins*win
    kc=T+256
    out=pl.pallas_call(functools.partial(corr_kernel,kc=kc,count=count),
        out_shape=jax.ShapeDtypeStruct((count,16,NLAG),f32),
        out_specs=pl.BlockSpec(memory_space=pltpu.HBM),
        scratch_shapes=[pltpu.VMEM((count,16,NLAG),f32),pltpu.SemaphoreType.DMA((count//SENT,)),pltpu.VMEM((16,T),bf16),pltpu.VMEM((4,16,T+768),bf16),pltpu.VMEM((2,16*(3*G//2+2),128),f32)],
        compiler_params=pltpu.CompilerParams(vmem_limit_bytes=36*1024*1024),
    )(x,other,*ready)
    return out


def shards(record, fir_taps, source_index):
    sections = lax.axis_size("sec")
    pair = sections == 2
    sources = source_index.shape[0]
    hbm = [pltpu.with_memory_space_constraint(x, pltpu.HBM) for x in (record, fir_taps, source_index)]
    exch = share(*hbm, pair)
    filt = filter_rows(record, fir_taps)
    if pair:
        others = (exch, lax.ppermute(exch, "sec", [(0, 1), (1, 0)]))
    else:
        pilots = lax.psum(exch[:sources], "sec")
        up = [(i, i + 1) for i in range(sections - 1)]
        down = [(i + 1, i) for i in range(sections - 1)]
        high = lax.ppermute(exch[sources : sources + HALO], "sec", down)
        low = lax.ppermute(exch[sources + HALO :], "sec", up)
        others = (pilots, low, high)
    blocks = pack(filt, others, lax.axis_size("tm"), sources, pair)
    blocks = lax.all_to_all(blocks, "tm", 0, 0, tiled=True)
    swap = [(i, i ^ 1) for i in range(lax.axis_size("tm"))]
    other = lax.ppermute(blocks[:, :HALF], "tm", swap)
    return correlate(blocks, other, make_ready(blocks))


def solution(mesh):
    in_specs = (P("sec", "tm"), P(), P())
    out_specs = P(("sec", "tm"), None, None)
    return jax.shard_map(shards, mesh=mesh, in_specs=in_specs, out_specs=out_specs, check_vma=False)
```
